32 devices in a mesh: tm: 8 (over y, x, core), panel: 4 (over z).
Axes of the slice: x: 2, y: 2, z: 4, core: 2. Of those that a mesh axis runs over, the one named last changes fastest.
Arguments:
- forward_element: bfloat16 [3, 8, 1024, 1024], P(None, 'tm', 'panel'), may hold values from -1 to 1
- backward_element: bfloat16 [3, 8, 1024, 1024], P(None, 'tm', 'panel'), may hold values from -1 to 1
Outputs:
- forward_joint: bfloat16 [3, 8, 1024, 1024], P(None, 'tm', 'panel')
- backward_joint: bfloat16 [3, 8, 1024, 1024], P(None, 'tm', 'panel')
The draws below stay inside these ranges and needn't reach their ends.
All inputs are finite; a program needn't handle non-finite values.
Results may differ from the reference program's by a relative error of at most 0.0067.
Values may be sent and summed in bfloat16 or wider, within the bound.
No kernel may reach another device: no remote copies, remote signals or barrier semaphores. Data moves between devices by JAX's collectives and lax.ppermute only.
A program may use at most 128 MiB of HBM per device.

```python
import math
import jax
import jax.numpy as jnp
from jax import lax

STATE = 1024
LEVELS = 2
GROUPS = 8


spread_scale = 0.28


def perturbation_field(field_key):
    values = jnp.clip(jax.random.normal(field_key, (GROUPS, STATE, STATE), jnp.float32), -4.0, 4.0)
    return values


def covariance_like(matrix_key):
    subkeys = jax.random.split(matrix_key, 2)
    perturbation = perturbation_field(subkeys[0]) * (spread_scale / math.sqrt(STATE))
    perturbation = (perturbation + jnp.swapaxes(perturbation, 1, 2)) * 0.7071
    diagonal = jnp.exp(jax.random.uniform(subkeys[1], (GROUPS, STATE), jnp.float32, math.log(0.15), math.log(0.5)))
    identity = jnp.eye(STATE, dtype=jnp.float32)
    return perturbation * (1.0 - identity) + identity * diagonal[:, :, None]


def transition_like(matrix_key):
    subkeys = jax.random.split(matrix_key, 2)
    perturbation = perturbation_field(subkeys[0]) * (0.3 / math.sqrt(STATE))
    diagonal = jax.random.uniform(subkeys[1], (GROUPS, STATE), jnp.float32, 0.5, 0.9)
    identity = jnp.eye(STATE, dtype=jnp.float32)
    return perturbation * (1.0 - identity) + identity * diagonal[:, :, None]


def assemble(element_key):
    subkeys = jax.random.split(element_key, 3)
    return jnp.stack([covariance_like(subkeys[0]), transition_like(subkeys[1]), covariance_like(subkeys[2])]).astype(jnp.bfloat16)


def draw_forward_element(key, part):
    return assemble(jax.random.fold_in(key, 101))


def draw_backward_element(key, part):
    return assemble(jax.random.fold_in(key, 202))


def setup_inputs(seed: int = 0) -> dict:
    keys = jax.random.split(jax.random.key(seed), 3)
    return {
        "forward_element": draw_forward_element(jax.random.fold_in(keys[2], 71), 0),
        "backward_element": draw_backward_element(jax.random.fold_in(keys[2], 71), 0),
    }


def matmul(left, right):
    return jnp.dot(left, right, preferred_element_type=jnp.float32)


def combine(partner_cov, partner_trans, partner_info_rows, local_trans, local_info, local_cov_rows, row_start):
    row_count = local_cov_rows.shape[0]
    width = local_trans.shape[0]
    identity = jnp.eye(width, dtype=jnp.float32)
    kernel = matmul(partner_cov, local_info).astype(jnp.bfloat16)
    first_iterate = (identity - kernel).astype(jnp.bfloat16)
    second_iterate = (identity + kernel - matmul(kernel, first_iterate)).astype(jnp.bfloat16)
    local_rows = lax.dynamic_slice_in_dim(local_trans, row_start, row_count, 0)
    factor = matmul(matmul(local_rows, first_iterate).astype(jnp.bfloat16), second_iterate).astype(jnp.bfloat16)
    joint_trans = matmul(factor, partner_trans).astype(jnp.bfloat16)
    middle = matmul(factor, partner_cov).astype(jnp.bfloat16)
    joint_cov = (lax.dot_general(middle, local_trans, (((1,), (1,)), ((), ())), preferred_element_type=jnp.float32) + local_cov_rows).astype(jnp.bfloat16)
    columns = lax.dynamic_slice_in_dim(partner_trans, row_start, row_count, 1)
    upper_rows = lax.dot_general(columns, local_info, (((0,), (0,)), ((), ())), preferred_element_type=jnp.float32).astype(jnp.bfloat16)
    upper_rows = matmul(upper_rows, first_iterate).astype(jnp.bfloat16)
    upper_rows = matmul(upper_rows, second_iterate).astype(jnp.bfloat16)
    joint_info = (matmul(upper_rows, partner_trans) + partner_info_rows).astype(jnp.bfloat16)
    return jnp.stack([joint_cov, joint_trans, joint_info])


def combine_whole(partner, local_element):
    return combine(partner[0], partner[1], partner[2], local_element[1], local_element[2], local_element[0], 0)


def reference(forward_element, backward_element):
    forward = [forward_element[:, position] for position in range(GROUPS)]
    backward = [backward_element[:, position] for position in range(GROUPS)]
    for level_index in range(LEVELS):
        stride = 1 << level_index
        forward = [combine_whole(forward[position - stride], forward[position]) if position >= stride else forward[position] for position in range(GROUPS)]
        backward = [combine_whole(backward[position + stride], backward[position]) if position + stride < GROUPS else backward[position] for position in range(GROUPS)]
    return jnp.stack(forward, axis=1), jnp.stack(backward, axis=1)
```

```python
import functools

import jax
import jax.numpy as jnp
from jax import lax
from jax.experimental import pallas as pl
from jax.experimental.pallas import tpu as pltpu
from jax.sharding import PartitionSpec as P

AXES = ("tm", "panel")
VMEM_BYTES = 60 * 2**20
ANY = pl.BlockSpec(memory_space=pl.ANY)


class Plan:
    def __init__(self, groups, panels):
        self.groups, self.panels, self.half = groups, panels, panels // 2
        assert groups % 2 == 0 and panels % 4 == 0
        columns = range(groups // 2)
        half = self.half

        def table(forward_routes):
            last = groups * panels - 1
            routes = [(a * panels + b, c * panels + d) for (a, b), (c, d) in forward_routes]
            return routes + [(last - source, last - target) for source, target in routes]

        def in_range(routes):
            return [route for route in routes if route[1][0] < groups]

        everyone = [(t, z) for t in range(groups) for z in range(panels)]
        self.cross = [(t * panels + z, t * panels + (z + half) % panels) for t, z in everyone]
        self.core = [(t * panels + z, (t ^ 1) * panels + z) for t, z in everyone]
        self.gather = {}
        for d in range(1, half):
            routes = []
            for c in columns:
                even, odd = 2 * c, 2 * c + 1
                routes += [((even, (layer + d) % half), (even, layer)) for layer in (0, 1)]
                routes += [((odd, (1 + d) % half), (odd, 1)), ((odd, d), (odd + 2, 0))]
            self.gather[d] = table(in_range(routes))
        self.onward = table(in_range([((2 * c + 1, 0), (2 * c + 3, 0)) for c in columns]))
        q_devices = [(2 * c + layer, layer) for c in columns for layer in (0, 1)]
        p_devices = [(2 * c + 1 - layer, layer) for c in columns for layer in (0, 1)]
        self.next_q = table(in_range([((t, z), (t + 2, z)) for t, z in q_devices]))
        self.next_all = table(in_range([((t, z), (t + 2, z)) for t, z in q_devices + p_devices]))
        self.home_q, self.home_all = [], []
        last_t, last_z = groups - 1, panels - 1
        for j in range(panels):
            q_routes, p_routes = [], []
            for t, z in q_devices:
                q_routes += [((t, z), (t, j)), ((last_t - t, last_z - z), (last_t - t, (j + half) % panels))]
            for t, z in p_devices:
                segment = t ^ 1 if (t % 2) != z else t
                p_routes += [
                    ((t, z), (segment, (j + 1) % panels)),
                    ((last_t - t, last_z - z), (last_t - segment, (j + half + 1) % panels)),
                ]
            flat = lambda routes: [(a * panels + b, c * panels + d) for (a, b), (c, d) in routes]
            self.home_q.append(flat(q_routes))
            self.home_all.append(flat(q_routes + p_routes))


class Place:
    def __init__(self, plan):
        t, z = lax.axis_index("tm"), lax.axis_index("panel")
        self.plan = plan
        self.z = z
        self.forward = z < plan.half
        self.layer = jnp.where(self.forward, z, plan.panels - 1 - z)
        self.t = jnp.where(self.forward, t, plan.groups - 1 - t)
        core = lax.rem(self.t, 2)
        self.is_q = lax.rem(core + self.layer, 2) == 0
        self.is_p = jnp.logical_not(self.is_q)
        self.special = jnp.logical_and(core == 1, self.layer == 0)
        self.segment = self.t - core + self.layer

    def source(self, d):
        layer = lax.rem(self.layer + d, self.plan.half)
        return jnp.where(self.forward, layer, self.plan.panels - 1 - layer)


def call(kernel, out_shapes, operands, scratch=(), flops=0, out_space=pl.ANY):
    moved = sum(x.size * x.dtype.itemsize for x in list(operands) + list(out_shapes))
    return pl.pallas_call(
        kernel,
        out_shape=list(out_shapes),
        in_specs=[ANY] * len(operands),
        out_specs=[pl.BlockSpec(memory_space=out_space)] * len(out_shapes),
        scratch_shapes=list(scratch),
        compiler_params=pltpu.CompilerParams(vmem_limit_bytes=VMEM_BYTES),
        cost_estimate=pl.CostEstimate(flops=flops, bytes_accessed=moved, transcendentals=0),
    )(*operands)


def bf16(*shape):
    return jax.ShapeDtypeStruct(shape, jnp.bfloat16)


def assemble_kernel(plan, kind, *refs):
    half = plan.half
    own, s1_q, s1_p, onward_local, onward_crossed = refs[:5]
    local, crossed = refs[5 : 5 + half - 1], refs[5 + half - 1 : 5 + 2 * (half - 1)]
    out, sems = refs[-2], refs[-1]
    place = Place(plan)
    rows = out.shape[0] // plan.panels
    index = {
        "A": 1,
        "first": jnp.where(place.is_q, 2, 0),
        "third": jnp.where(place.is_q, 0, 2),
    }[kind]

    def target(block):
        return out.at[pl.ds(pl.multiple_of(block * rows, rows), rows), :]

    def put(source, block, sem):
        return pltpu.make_async_copy(source, target(block), sems.at[sem])

    ordinary = jnp.logical_not(place.special)
    here = place.source(0)
    there = lax.rem(here + half, plan.panels)
    pl.when(ordinary)(lambda: put(own.at[index], here, 0).start())
    pl.when(place.special)(lambda: put(onward_local.at[index], here, 0).start())
    pl.when(jnp.logical_and(ordinary, place.is_q))(lambda: put(s1_q, there, 1).start())
    pl.when(jnp.logical_and(ordinary, place.is_p))(lambda: put(s1_p, there, 1).start())
    pl.when(place.special)(lambda: put(onward_crossed, there, 1).start())
    rest = []
    for d in range(1, half):
        block = place.source(d)
        rest.append(put(local[d - 1].at[index], block, 2 * d))
        rest.append(put(crossed[d - 1], lax.rem(block + half, plan.panels), 2 * d + 1))
    for copy in rest:
        copy.start()
    put(s1_q, here, 0).wait()
    put(s1_q, there, 1).wait()
    for copy in rest:
        copy.wait()


def dot(a, b):
    return jnp.dot(a, b, preferred_element_type=jnp.float32)


def dot_dims(a, b, dims):
    return lax.dot_general(a, b, (dims, ((), ())), preferred_element_type=jnp.float32)


def identity(n):
    return (
        lax.broadcasted_iota(jnp.int32, (n, n), 0) == lax.broadcasted_iota(jnp.int32, (n, n), 1)
    ).astype(jnp.float32)


def store_blocks(plan, place, shift, result, outs, sems, condition):
    rows = result.shape[0] // plan.panels
    if len(outs) == 1:
        copies = [pltpu.make_async_copy(result, outs[0], sems.at[0])]
    else:
        base = jnp.where(place.forward, 0, plan.half) + shift
        copies = []
        for j, out in enumerate(outs):
            block = lax.rem(base + j, plan.panels)
            source = result.at[pl.ds(pl.multiple_of(block * rows, rows), rows), :]
            copies.append(pltpu.make_async_copy(source, out, sems.at[j]))

    def run():
        for copy in copies:
            copy.start()
        for copy in copies:
            copy.wait()

    pl.when(condition)(run)


def first_kernel(plan, stride, cp_q, jq_q, cp_p, jq_p, aq_ref, cq_ref, *refs):
    count = len(refs) - 10
    outs, (v_ref, r_ref) = refs[:count], refs[count : count + 2]
    cp, jq, aq, cq, x1, r, u, sems = refs[count + 2 :]
    place = Place(plan)
    usable = place.segment >= stride
    n = cp.shape[0]

    def fetch(source, target, i):
        return pltpu.make_async_copy(source, target, sems.at[i])

    @pl.when(place.is_q)
    def _():
        fetch(cp_q, cp, 0).start()
        fetch(jq_q, jq, 1).start()
        fetch(aq_ref, aq, 2).start()
        fetch(cq_ref, cq, 3).start()

    @pl.when(place.is_p)
    def _():
        fetch(cp_p, cp, 0).start()
        fetch(jq_p, jq, 1).start()

    fetch(cp_q, cp, 0).wait()
    fetch(jq_q, jq, 1).wait()

    @pl.when(usable)
    def _():
        u[...] = dot(cp[...], jq[...]).astype(jnp.bfloat16)
        x1[...] = (identity(n) - u[...]).astype(jnp.bfloat16)
        r[...] = (identity(n) + u[...] - dot(u[...], x1[...])).astype(jnp.bfloat16)

    @pl.when(place.is_q)
    def _():
        fetch(aq_ref, aq, 2).wait()
        fetch(cq_ref, cq, 3).wait()

    @pl.when(jnp.logical_and(usable, place.is_q))
    def _():
        u[...] = dot(aq[...], x1[...]).astype(jnp.bfloat16)
        x1[...] = dot(u[...], r[...]).astype(jnp.bfloat16)
        u[...] = dot(x1[...], cp[...]).astype(jnp.bfloat16)
        cq[...] = (dot_dims(u[...], aq[...], ((1,), (1,))) + cq[...]).astype(jnp.bfloat16)

    fetch(x1, v_ref, 0).start()
    fetch(r, r_ref, 1).start()
    store_blocks(plan, place, 0, cq, outs, sems.at[pl.ds(2, plan.panels)], place.is_q)
    fetch(x1, v_ref, 0).wait()
    fetch(r, r_ref, 1).wait()


def second_kernel(plan, stride, ap_q, ap_p, v_ref, r_ref, aq_ref, jq_ref, jp_ref, *refs):
    outs = refs[:-6]
    ap, v, r, jq, jp, sems = refs[-6:]
    place = Place(plan)
    usable = place.segment >= stride

    def fetch(source, target, i):
        return pltpu.make_async_copy(source, target, sems.at[i])

    @pl.when(place.is_q)
    def _():
        fetch(ap_q, ap, 0).start()
        fetch(v_ref, v, 1).start()
        fetch(aq_ref, jq, 2).start()

    @pl.when(place.is_p)
    def _():
        fetch(ap_p, ap, 0).start()
        fetch(v_ref, v, 1).start()
        fetch(jq_ref, jq, 2).start()
        fetch(r_ref, r, 3).start()
        fetch(jp_ref, jp, 4).start()

    fetch(ap_q, ap, 0).wait()
    fetch(v_ref, v, 1).wait()
    fetch(jq_ref, jq, 2).wait()

    @pl.when(place.is_p)
    def _():
        fetch(r_ref, r, 3).wait()
        fetch(jp_ref, jp, 4).wait()

    @pl.when(jnp.logical_and(usable, place.is_q))
    def _():
        jq[...] = dot(v[...], ap[...]).astype(jnp.bfloat16)

    @pl.when(jnp.logical_and(usable, place.is_p))
    def _():
        jq[...] = dot_dims(ap[...], jq[...], ((0,), (0,))).astype(jnp.bfloat16)
        v[...] = dot(jq[...], v[...]).astype(jnp.bfloat16)
        r[...] = dot(v[...], r[...]).astype(jnp.bfloat16)
        jq[...] = (dot(r[...], ap[...]) + jp[...]).astype(jnp.bfloat16)

    store_blocks(plan, place, jnp.where(place.is_q, 0, 1), jq, outs, sems, place.layer >= 0)


def home_kernel(plan, *refs):
    panels, half = plan.panels, plan.half
    c_rounds, aj_rounds = refs[:panels], refs[panels : 2 * panels]
    f_out, b_out, sems = refs[2 * panels :]
    z = lax.axis_index("panel")
    parts = [
        (c_rounds, 0, f_out.at[0]),
        (aj_rounds, 0, f_out.at[1]),
        (aj_rounds, 1, f_out.at[2]),
        (c_rounds, half, b_out.at[0]),
        (aj_rounds, half, b_out.at[1]),
        (aj_rounds, half + 1, b_out.at[2]),
    ]
    for i, (rounds, shift, target) in enumerate(parts):
        which = lax.rem(z - shift + 2 * panels, panels)
        for j, block in enumerate(rounds):
            pl.when(which == j)(pltpu.make_async_copy(block, target, sems.at[i]).start)
    for i, (rounds, shift, target) in enumerate(parts):
        pltpu.make_async_copy(rounds[0], target, sems.at[i]).wait()


def shards(plan, forward_element, backward_element):
    forward, backward = forward_element[:, 0], backward_element[:, 0]
    rows, n = forward.shape[1:]
    panels, half = plan.panels, plan.half
    full, block = bf16(n, n), bf16(rows, n)
    square = pltpu.VMEM((n, n), jnp.bfloat16)
    dma = pltpu.SemaphoreType.DMA

    def send(x, routes):
        return lax.ppermute(x, AXES, routes)

    t, z = lax.axis_index("tm"), lax.axis_index("panel")
    layer = jnp.where(z < half, z, panels - 1 - z)
    core = jnp.where(z < half, t, plan.groups - 1 - t) % 2
    to_q = {d: layer == (core + d) % half for d in range(1, half)}
    own = jnp.where(z < half, forward, backward)
    other_c, other_a, other_j = [jnp.where(z < half, backward[i], forward[i]) for i in range(3)]

    s1_a = send(other_a, plan.cross)
    s1_c = send(other_c, plan.cross)
    s1_j = send(other_j, plan.cross)
    steps = range(1, half)
    local = [send(own, plan.gather[d]) for d in steps]
    onward_local = send(own, plan.onward)
    crossed_a = [send(s1_a, plan.gather[d]) for d in steps]
    onward_a = send(s1_a, plan.onward)
    crossed_first = [send(jnp.where(to_q[d], s1_j, s1_c), plan.gather[d]) for d in steps]
    onward_first = send(s1_c, plan.onward)
    crossed_third = [send(jnp.where(to_q[d], s1_c, s1_j), plan.gather[d]) for d in steps]
    onward_third = send(s1_j, plan.onward)

    def assemble(kind, s1_q, s1_p, onward_crossed, crossed):
        return call(
            functools.partial(assemble_kernel, plan, kind),
            [full],
            [own, s1_q, s1_p, onward_local, onward_crossed, *local, *crossed],
            [dma((panels,))],
            out_space=pltpu.VMEM,
        )[0]

    a_own = assemble("A", s1_a, s1_a, onward_a, crossed_a)
    a_swap = send(a_own, plan.core)
    first_own = assemble("first", s1_j, s1_c, onward_first, crossed_first)
    first_swap = send(first_own, plan.core)
    third = assemble("third", s1_c, s1_j, onward_third, crossed_third)

    def first(stride, outs, cp_q, jq_q, cp_p, jq_p, aq, cq):
        return call(
            functools.partial(first_kernel, plan, stride),
            [*outs, full, full],
            [cp_q, jq_q, cp_p, jq_p, aq, cq],
            [square] * 7 + [dma((2 + panels,))],
            flops=12 * n**3,
        )

    def second(stride, outs, ap_q, ap_p, v, r, aq, jq, jp):
        return call(
            functools.partial(second_kernel, plan, stride),
            outs,
            [ap_q, ap_p, v, r, aq, jq, jp],
            [square] * 5 + [dma((max(5, panels),))],
            flops=8 * n**3,
        )

    c_new, v, r = first(1, [full], first_swap, first_own, first_own, first_swap, a_own, third)
    c_next = send(c_new, plan.next_q)
    (aj_new,) = second(1, [full], a_swap, a_own, v, r, a_own, first_swap, third)
    aj_next = send(aj_new, plan.next_all)
    aj_swap = send(aj_new, plan.core)
    c_next_swap = send(c_next, plan.core)

    *c_blocks, v, r = first(2, [block] * panels, c_next, aj_swap, c_next_swap, aj_new, aj_new, c_new)
    c_home = [send(x, routes) for x, routes in zip(c_blocks, plan.home_q)]
    aj_next_swap = send(aj_next, plan.core)
    aj_blocks = second(2, [block] * panels, aj_next, aj_next_swap, v, r, aj_new, aj_new, aj_next)
    aj_home = [send(x, routes) for x, routes in zip(aj_blocks, plan.home_all)]

    f_out, b_out = call(
        functools.partial(home_kernel, plan),
        [bf16(3, rows, n)] * 2,
        [*c_home, *aj_home],
        [dma((6,))],
        out_space=pltpu.VMEM,
    )
    return f_out[:, None], b_out[:, None]


def solution(mesh):
    plan = Plan(mesh.shape["tm"], mesh.shape["panel"])
    spec = P(None, "tm", "panel", None)
    return jax.shard_map(
        functools.partial(shards, plan),
        mesh=mesh,
        in_specs=(spec, spec),
        out_specs=(spec, spec),
        check_vma=False,
    )
```

```python
import functools

import jax
import jax.numpy as jnp
from jax import lax
from jax.experimental import pallas as pl
from jax.experimental.pallas import tpu as pltpu
from jax.sharding import PartitionSpec as P

AXES = ("tm", "panel")
VMEM_BYTES = 60 * 2**20
TILE = 512
HBM = pl.BlockSpec(memory_space=pltpu.HBM)


class Plan:
    def __init__(self, groups, panels):
        self.groups, self.panels, self.half = groups, panels, panels // 2
        assert groups % 2 == 0 and panels % 4 == 0
        columns = range(groups // 2)
        half = self.half

        def table(forward_routes):
            last = groups * panels - 1
            routes = [(a * panels + b, c * panels + d) for (a, b), (c, d) in forward_routes]
            return routes + [(last - source, last - target) for source, target in routes]

        def in_range(routes):
            return [route for route in routes if route[1][0] < groups]

        everyone = [(t, z) for t in range(groups) for z in range(panels)]
        self.cross = [(t * panels + z, t * panels + (z + half) % panels) for t, z in everyone]
        self.core = [(t * panels + z, (t ^ 1) * panels + z) for t, z in everyone]
        self.gather = {}
        for d in range(1, half):
            routes = []
            for c in columns:
                even, odd = 2 * c, 2 * c + 1
                routes += [((even, (layer + d) % half), (even, layer)) for layer in (0, 1)]
                routes += [((odd, (1 + d) % half), (odd, 1)), ((odd, d), (odd + 2, 0))]
            self.gather[d] = table(in_range(routes))
        self.onward = table(in_range([((2 * c + 1, 0), (2 * c + 3, 0)) for c in columns]))
        q_devices = [(2 * c + layer, layer) for c in columns for layer in (0, 1)]
        p_devices = [(2 * c + 1 - layer, layer) for c in columns for layer in (0, 1)]
        self.next_q, self.next_p = [
            table(in_range([((t, z), (t + 2, z)) for t, z in devices])) for devices in (q_devices, p_devices)
        ]
        self.home_q, self.home_p = [], []
        last_t, last_z = groups - 1, panels - 1
        for j in range(panels):
            for devices, shift, rounds in ((q_devices, 0, self.home_q), (p_devices, 1, self.home_p)):
                routes = []
                for t, z in devices:
                    segment = t - t % 2 + z
                    routes.append((t * panels + z, segment * panels + (z + j + shift) % panels))
                    t, z, segment = last_t - t, last_z - z, last_t - segment
                    routes.append((t * panels + z, segment * panels + (z + j + shift) % panels))
                rounds.append(routes)


class Place:
    def __init__(self, plan):
        t, z = lax.axis_index("tm"), lax.axis_index("panel")
        self.plan = plan
        self.z = z
        self.forward = z < plan.half
        self.layer = jnp.where(self.forward, z, plan.panels - 1 - z)
        self.t = jnp.where(self.forward, t, plan.groups - 1 - t)
        core = lax.rem(self.t, 2)
        self.is_q = lax.rem(core + self.layer, 2) == 0
        self.is_p = jnp.logical_not(self.is_q)
        self.special = jnp.logical_and(core == 1, self.layer == 0)
        self.segment = self.t - core + self.layer

    def source(self, d):
        layer = lax.rem(self.layer + d, self.plan.half)
        return jnp.where(self.forward, layer, self.plan.panels - 1 - layer)


def call(kernel, out_shapes, operands, scratch=(), out_space=pltpu.HBM, flops=1):
    return pl.pallas_call(
        kernel,
        out_shape=list(out_shapes),
        in_specs=[HBM] * len(operands),
        out_specs=[pl.BlockSpec(memory_space=out_space)] * len(out_shapes),
        scratch_shapes=list(scratch),
        compiler_params=pltpu.CompilerParams(vmem_limit_bytes=VMEM_BYTES),
        cost_estimate=pl.CostEstimate(flops=flops, bytes_accessed=1, transcendentals=0),
    )(*operands)


def bf16(*shape):
    return jax.ShapeDtypeStruct(shape, jnp.bfloat16)


def whole(plan, place, kind, near, far, target, sems):
    half = plan.half
    own, onward_local, *local = near
    s1, onward_far, *gathered = far
    rows = target.shape[0] // plan.panels
    index = {"first": jnp.where(place.is_q, 2, 0), "A": 1, "third": jnp.where(place.is_q, 0, 2)}[kind]
    part = {"first": lambda x: x, "A": lambda x: x.at[0], "third": lambda x: x.at[1]}[kind]

    def put(source, block, sem):
        rows_there = target.at[pl.ds(pl.multiple_of(block * rows, rows), rows), :]
        return pltpu.make_async_copy(source, rows_there, sems.at[sem])

    copies = []
    for d in range(half):
        block = place.source(d)
        beyond = lax.rem(block + half, plan.panels)
        here, there = (own, s1.at[index]) if d == 0 else (local[d - 1], part(gathered[d - 1]))
        copies += [put(here.at[index], block, 2 * d), put(there, beyond, 2 * d + 1)]
        if d == 0:
            special = [put(onward_local.at[index], block, 0), put(part(onward_far), beyond, 1)]

    def start():
        @pl.when(place.special)
        def _():
            for copy in special:
                copy.start()

        @pl.when(jnp.logical_not(place.special))
        def _():
            for copy in copies[:2]:
                copy.start()

        for copy in copies[2:]:
            copy.start()

    def wait():
        for copy in copies:
            copy.wait()

    return start, wait


def split_raw(plan, refs):
    return refs[: 1 + plan.half], refs[1 + plan.half : 2 + 2 * plan.half], refs[2 + 2 * plan.half :]


def assemble_kernel(plan, kind, *refs):
    near, far, (out, sems) = split_raw(plan, refs)
    start, wait = whole(plan, Place(plan), kind, near, far, out, sems)
    start()
    wait()


def product(out, a, b, finish=lambda acc, rows: acc, a_transposed=False, b_transposed=False, tile=TILE):
    n = out.shape[0]
    tile = min(tile, n)
    dims = (((0 if a_transposed else 1,), (1 if b_transposed else 0,)), ((), ()))

    @pl.loop(0, n // tile)
    def _(i):
        rows = pl.ds(pl.multiple_of(i * tile, tile), tile)
        left = a[:, rows] if a_transposed else a[rows, :]
        acc = lax.dot_general(left, b[...], dims, preferred_element_type=jnp.float32)
        out[rows, :] = finish(acc, rows).astype(jnp.bfloat16)


def identity(rows, n):
    shape = (rows.size, n)
    row = lax.broadcasted_iota(jnp.int32, shape, 0) + rows.start
    return (row == lax.broadcasted_iota(jnp.int32, shape, 1)).astype(jnp.float32)


def both(place, sems, sem, source_q, source_p, target):
    copy_q = pltpu.make_async_copy(source_q, target, sems.at[sem])
    copy_p = pltpu.make_async_copy(source_p, target, sems.at[sem])
    pl.when(place.is_q)(copy_q.start)
    pl.when(place.is_p)(copy_p.start)
    return copy_q.wait


def block_copies(plan, place, shift, result, outs, sems):
    rows = result.shape[0] // plan.panels
    base = place.z + shift
    copies = []
    for j, out in enumerate(outs):
        block = lax.rem(base + j, plan.panels)
        source = result.at[pl.ds(pl.multiple_of(block * rows, rows), rows), :]
        copies.append(pltpu.make_async_copy(source, out, sems.at[j]))
    return copies


def run(condition, copies):
    @pl.when(condition)
    def _():
        for copy in copies:
            copy.start()
        for copy in copies:
            copy.wait()


def iterates(n, cp, jq, u, x1, r):
    def first_iterate(acc, rows):
        x1[rows, :] = (identity(rows, n) - acc.astype(jnp.bfloat16)).astype(jnp.bfloat16)
        return acc

    product(u, cp, jq, first_iterate, tile=n)
    product(r, u, x1, lambda acc, rows: identity(rows, n) + u[rows, :] - acc, tile=n)


def iterate_kernel(plan, stride, *refs):
    half = plan.half
    mine, theirs = refs[: 1 + half], refs[1 + half : 2 + 2 * half]
    x1_ref, r_ref, other_ref, cp, jq, u, x1, r, sems = refs[2 + 2 * half :]
    place = Place(plan)
    rows = cp.shape[0] // plan.panels

    def copies(parts, target, first_sem):
        near, *far = parts
        result = []
        for d in range(half):
            block = place.source(d)
            for source, at in ((near.at[d], block), (far[d], lax.rem(block + half, plan.panels))):
                there = target.at[pl.ds(pl.multiple_of(at * rows, rows), rows), :]
                result.append(pltpu.make_async_copy(source, there, sems.at[first_sem + len(result)]))
        return result

    to_q = copies(theirs, cp, 0) + copies(mine, jq, plan.panels)
    to_p = copies(mine, cp, 0) + copies(theirs, jq, plan.panels)
    for condition, loads in ((place.is_q, to_q), (place.is_p, to_p)):
        @pl.when(condition)
        def _():
            for copy in loads:
                copy.start()

    for copy in to_q:
        copy.wait()
    store_q = pltpu.make_async_copy(cp, other_ref, sems.at[0])
    store_p = pltpu.make_async_copy(jq, other_ref, sems.at[0])
    pl.when(place.is_q)(store_q.start)
    pl.when(place.is_p)(store_p.start)

    @pl.when(place.segment >= stride)
    def _():
        iterates(cp.shape[0], cp, jq, u, x1, r)

    run(place.layer >= 0, [pltpu.make_async_copy(x1, x1_ref, sems.at[1]), pltpu.make_async_copy(r, r_ref, sems.at[2])])
    store_q.wait()


def combine_kernel(plan, stride, cp_ref, x1_ref, r_ref, jq_ref, *refs):
    near, far, refs = split_raw(plan, refs)
    cj_ref, v_ref, a, x1, r, jc, u, w, third, sems, a_sems, third_sems = refs
    place = Place(plan)
    usable = place.segment >= stride
    start_a, wait_a = whole(plan, place, "A", near, far, a, a_sems)
    start_third, wait_third = whole(plan, place, "third", near, far, third, third_sems)
    start_a()
    wait_jc = both(place, sems, 0, cp_ref, jq_ref, jc)
    load_x1 = pltpu.make_async_copy(x1_ref, x1, sems.at[1])
    load_r = pltpu.make_async_copy(r_ref, r, sems.at[2])
    load_x1.start()
    load_r.start()
    start_third()
    wait_a()

    @pl.when(place.is_q)
    def _():
        load_x1.wait()
        load_r.wait()

        @pl.when(usable)
        def _():
            product(u, a, x1)
            product(w, u, r)

        store_v = pltpu.make_async_copy(w, v_ref, sems.at[3])
        store_v.start()
        wait_jc()

        @pl.when(usable)
        def _():
            product(u, w, jc)

        wait_third()

        @pl.when(usable)
        def _():
            product(third, u, a, lambda acc, rows: acc + third[rows, :], b_transposed=True)

        run(place.is_q, [pltpu.make_async_copy(third, cj_ref, sems.at[4])])
        store_v.wait()

    @pl.when(place.is_p)
    def _():
        wait_jc()

        @pl.when(usable)
        def _():
            product(u, a, jc, a_transposed=True)

        load_x1.wait()
        load_r.wait()

        @pl.when(usable)
        def _():
            product(w, u, x1)
            product(u, w, r)

        wait_third()

        @pl.when(usable)
        def _():
            product(jc, u, a, lambda acc, rows: acc + third[rows, :])

        run(place.is_p, [pltpu.make_async_copy(jc, cj_ref, sems.at[4])])


def factor_kernel(plan, stride, v_ref, ap_ref, aq_ref, out, v, ap, sems):
    place = Place(plan)
    usable = place.segment >= stride

    @pl.when(place.is_q)
    def _():
        loads = [pltpu.make_async_copy(v_ref, v, sems.at[0]), pltpu.make_async_copy(ap_ref, ap, sems.at[1])]
        run(usable, loads)

        @pl.when(usable)
        def _():
            product(v, v, ap)

        run(jnp.logical_not(usable), [pltpu.make_async_copy(aq_ref, v, sems.at[0])])
        run(place.is_q, [pltpu.make_async_copy(v, out, sems.at[2])])


def front_kernel(plan, stride, cp_q, jq_q, cp_p, jq_p, aq_ref, cq_ref, *refs):
    blocks = refs[: plan.panels]
    v_ref, r_ref, cp, jq, aq, x1, r, u, cq, sems = refs[plan.panels :]
    place = Place(plan)
    usable = place.segment >= stride
    n = cp.shape[0]

    wait_cp = both(place, sems, 0, cp_q, cp_p, cp)
    wait_jq = both(place, sems, 1, jq_q, jq_p, jq)
    load_aq = pltpu.make_async_copy(aq_ref, aq, sems.at[2])
    load_cq = pltpu.make_async_copy(cq_ref, cq, sems.at[3])
    pl.when(place.is_q)(load_aq.start)
    pl.when(place.is_q)(load_cq.start)
    wait_cp()
    wait_jq()

    @pl.when(usable)
    def _():
        iterates(n, cp, jq, u, x1, r)

    store_v = pltpu.make_async_copy(x1, v_ref, sems.at[0])
    store_r = pltpu.make_async_copy(r, r_ref, sems.at[1])

    @pl.when(place.is_p)
    def _():
        run(place.is_p, [store_v, store_r])

    @pl.when(place.is_q)
    def _():
        load_aq.wait()

        @pl.when(usable)
        def _():
            product(u, aq, x1, tile=n)
            product(x1, u, r, tile=n)

        store_v.start()

        @pl.when(usable)
        def _():
            product(u, x1, cp, tile=n)

        load_cq.wait()

        @pl.when(usable)
        def _():
            product(cq, u, aq, lambda acc, rows: acc + cq[rows, :], b_transposed=True, tile=n)

        run(place.is_q, block_copies(plan, place, 0, cq, blocks, sems.at[pl.ds(4, plan.panels)]))
        store_v.wait()


def trans_kernel(plan, stride, ap_q, ap_p, v_ref, r_ref, aq_ref, jq_ref, *refs):
    blocks = refs[: plan.panels]
    h_ref, ap, v, r, jq, u, sems = refs[plan.panels :]
    place = Place(plan)
    usable = place.segment >= stride
    wait_ap = both(place, sems, 0, ap_q, ap_p, ap)
    wait_jq = both(place, sems, 1, aq_ref, jq_ref, jq)
    load_v = pltpu.make_async_copy(v_ref, v, sems.at[2])
    load_r = pltpu.make_async_copy(r_ref, r, sems.at[3])
    load_v.start()
    pl.when(place.is_p)(load_r.start)
    wait_ap()
    wait_jq()

    @pl.when(place.is_q)
    def _():
        load_v.wait()

        @pl.when(usable)
        def _():
            product(jq, v, ap)

    run(place.is_q, block_copies(plan, place, 0, jq, blocks, sems.at[pl.ds(4, plan.panels)]))

    @pl.when(place.is_p)
    def _():
        @pl.when(usable)
        def _():
            product(u, ap, jq, a_transposed=True)

        load_v.wait()

        @pl.when(usable)
        def _():
            product(jq, u, v)

        load_r.wait()

        @pl.when(usable)
        def _():
            product(u, jq, r)

    run(place.is_p, [pltpu.make_async_copy(u, h_ref, sems.at[0])])


def info_kernel(plan, stride, h_ref, ap_ref, jp_ref, jq_ref, *refs):
    blocks = refs[: plan.panels]
    h, ap, jp, sems = refs[plan.panels :]
    place = Place(plan)
    usable = place.segment >= stride

    @pl.when(place.is_p)
    def _():
        pairs = [(h_ref, h), (ap_ref, ap), (jp_ref, jp)]
        loads = [pltpu.make_async_copy(s, d, sems.at[i]) for i, (s, d) in enumerate(pairs)]
        load_jq = pltpu.make_async_copy(jq_ref, jp, sems.at[2])

        @pl.when(usable)
        def _():
            for copy in loads:
                copy.start()
            for copy in loads:
                copy.wait()
            product(jp, h, ap, lambda acc, rows: acc + jp[rows, :])

        run(jnp.logical_not(usable), [load_jq])

    run(place.is_p, block_copies(plan, place, 1, jp, blocks, sems.at[pl.ds(3, plan.panels)]))


def home_kernel(plan, *refs):
    panels = plan.panels
    c_rounds, a_rounds, j_rounds = [refs[i * panels : (i + 1) * panels] for i in range(3)]
    f_out, b_out, sems = refs[3 * panels :]
    t, z = lax.axis_index("tm"), lax.axis_index("panel")
    forward_source = lax.rem(t, 2)
    backward_source = panels - 1 - lax.rem(plan.groups - 1 - t, 2)
    waits = []
    for out, source in ((f_out, forward_source), (b_out, backward_source)):
        for i, (rounds, shift) in enumerate(((c_rounds, 0), (a_rounds, 0), (j_rounds, 1))):
            which = lax.rem(z - source - shift + 2 * panels, panels)
            sem = sems.at[len(waits)]
            for j, block in enumerate(rounds):
                pl.when(which == j)(pltpu.make_async_copy(block, out.at[i], sem).start)
            waits.append(pltpu.make_async_copy(rounds[0], out.at[i], sem))
    for copy in waits:
        copy.wait()


def after(x, *others):
    return lax.optimization_barrier((x, *others))[0]


def shards(plan, forward_element, backward_element):
    forward, backward = forward_element[:, 0], backward_element[:, 0]
    rows, n = forward.shape[1:]
    panels, half = plan.panels, plan.half
    full, block = bf16(n, n), bf16(rows, n)
    square = pltpu.VMEM((n, n), jnp.bfloat16)
    dma = pltpu.SemaphoreType.DMA

    def send(x, routes):
        return lax.ppermute(x, AXES, routes)

    def kernel(body, *static):
        return functools.partial(body, plan, *static)

    t, z = lax.axis_index("tm"), lax.axis_index("panel")
    layer = jnp.where(z < half, z, panels - 1 - z)
    core = jnp.where(z < half, t, plan.groups - 1 - t) % 2
    to_q = {d: layer == (core + d) % half for d in range(1, half)}
    own = jnp.where(z < half, forward, backward)
    other = jnp.where(z < half, backward, forward)

    steps = range(1, half)
    s1 = send(other, plan.cross)
    local = [send(own, plan.gather[d]) for d in steps]
    onward_local = send(own, plan.onward)
    s1 = after(s1, onward_local, *local)
    gathered_first = [send(jnp.where(to_q[d], s1[2], s1[0]), plan.gather[d]) for d in steps]
    onward_first = send(s1[0], plan.onward)
    s1 = after(s1, onward_first)
    gathered_rest = [
        send(jnp.stack([s1[1], jnp.where(to_q[d], s1[0], s1[2])]), plan.gather[d]) for d in steps
    ]
    onward_rest = send(s1[1:], plan.onward)
    near = [own, onward_local, *local]

    is_q, special = (core + layer) % 2 == 0, (core == 1) & (layer == 0)

    def first_of(x):
        return jnp.where(is_q, x[2], x[0])

    early = jnp.stack([jnp.where(special, onward_local[0], first_of(own)), *map(first_of, local)])
    late = [jnp.where(special, onward_first, first_of(s1)), *gathered_first]
    x1, r, first_swap = call(
        kernel(iterate_kernel, 1),
        [full] * 3,
        [early, *late, send(early, plan.core), *[send(x, plan.core) for x in late]],
        [square] * 5 + [dma((2 * panels,))],
    )
    far_rest = [after(s1, x1), onward_rest, *gathered_rest]
    (a_own,) = call(
        kernel(assemble_kernel, "A"), [full], [*near, *far_rest], [dma((panels,))], out_space=pltpu.VMEM
    )
    a_swap = send(a_own, plan.core)
    cj_new, v = call(
        kernel(combine_kernel, 1),
        [full] * 2,
        [first_swap, after(x1, a_own), r, first_swap, *near, *far_rest],
        [square] * 7 + [dma((5,)), dma((panels,)), dma((panels,))],
    )
    c_next = send(cj_new, plan.next_q)
    j_swap = send(cj_new, plan.core)
    (a_new,) = call(
        kernel(factor_kernel, 1), [full], [v, after(a_swap, cj_new), a_own], [square] * 2 + [dma((3,))], flops=2 * n**3
    )
    c_next_swap = send(after(c_next, a_new), plan.core)
    a_next = send(after(a_new, c_next), plan.next_q)
    j_next = send(after(cj_new, c_next_swap), plan.next_p)

    *c_blocks, v, r = call(
        kernel(front_kernel, 2),
        [block] * panels + [full] * 2,
        [c_next, j_swap, c_next_swap, cj_new, a_new, cj_new],
        [square] * 7 + [dma((4 + panels,))],
    )
    c_home = [send(x, routes) for x, routes in zip(c_blocks[1:], plan.home_q[1:])]
    a_next = after(a_next, v, c_home[0])
    a_next_swap = send(a_next, plan.core)
    *a_blocks, h = call(
        kernel(trans_kernel, 2),
        [block] * panels + [full],
        [a_next, a_next_swap, v, r, a_new, cj_new],
        [square] * 5 + [dma((4 + panels,))],
    )
    a_home = [send(x, routes) for x, routes in zip(a_blocks[1:], plan.home_q[1:])]
    j_blocks = call(
        kernel(info_kernel, 2),
        [block] * panels,
        [h, a_next_swap, after(j_next, h, *c_home, a_home[0]), cj_new],
        [square] * 3 + [dma((3 + panels,))],
    )
    j_home = [send(x, routes) for x, routes in zip(j_blocks, plan.home_p)]

    f_out, b_out = call(
        kernel(home_kernel),
        [bf16(3, rows, n)] * 2,
        [c_blocks[0], *c_home, a_blocks[0], *a_home, *j_home],
        [dma((6,))],
        out_space=pltpu.VMEM,
    )
    return f_out[:, None], b_out[:, None]


def solution(mesh):
    plan = Plan(mesh.shape["tm"], mesh.shape["panel"])
    spec = P(None, "tm", "panel", None)
    return jax.shard_map(
        functools.partial(shards, plan),
        mesh=mesh,
        in_specs=(spec, spec),
        out_specs=(spec, spec),
        check_vma=False,
    )
```

```python
import functools

import jax
import jax.numpy as jnp
from jax import lax
from jax.experimental import pallas as pl
from jax.experimental.pallas import tpu as pltpu
from jax.sharding import PartitionSpec as P

AXES = ("tm", "panel")
VMEM_BYTES = 60 * 2**20
TILE = 512
HBM = pl.BlockSpec(memory_space=pltpu.HBM)


class Plan:
    def __init__(self, groups, panels):
        self.groups, self.panels, self.half = groups, panels, panels // 2
        assert groups % 2 == 0 and panels % 4 == 0
        columns = range(groups // 2)
        half = self.half

        def table(forward_routes):
            last = groups * panels - 1
            routes = [(a * panels + b, c * panels + d) for (a, b), (c, d) in forward_routes]
            return routes + [(last - source, last - target) for source, target in routes]

        def in_range(routes):
            return [route for route in routes if route[1][0] < groups]

        everyone = [(t, z) for t in range(groups) for z in range(panels)]
        self.core = [(t * panels + z, (t ^ 1) * panels + z) for t, z in everyone]
        q_of = {t: (t, t % 2) for t in range(groups)}
        p_of = {t: (t, 1) if t % 2 == 0 else (t + 2, 0) for t in range(groups)}
        self.cross = [table([((t, half + q), q_of[t]) for t in range(groups)]) for q in range(half)]
        self.forward = table(in_range([(q_of[t], p_of[t]) for t in range(groups)]))
        self.gather = {}
        for d in range(1, half):
            routes = [((t, (q_of[t][1] + d) % half), q_of[t]) for t in range(groups)]
            routes += [((t, (p_of[t][1] + d) % half), p_of[t]) for t in range(groups)]
            self.gather[d] = table(in_range(routes))
        self.onward = table(in_range([((t, 0), p_of[t]) for t in range(1, groups, 2)]))
        active = [(2 * c + core, layer) for c in columns for core in (0, 1) for layer in (0, 1)]
        self.next = table(in_range([((t, z), (t + 2, z)) for t, z in active]))
        self.home = {}
        for far in (True, False):
            for i in range(half // 2):
                routes = []
                for t, z in active:
                    d = i + (half // 2 if (t + z) % 2 == 0 else 0)
                    routes.append(((t, z), (t - t % 2 + z, half + d if far else (z + d) % half)))
                self.home[far, i] = table(routes)


class Place:
    def __init__(self, plan):
        t, z = lax.axis_index("tm"), lax.axis_index("panel")
        self.plan = plan
        self.forward = z < plan.half
        self.layer = jnp.where(self.forward, z, plan.panels - 1 - z)
        self.t = jnp.where(self.forward, t, plan.groups - 1 - t)
        core = lax.rem(self.t, 2)
        self.is_q = lax.rem(core + self.layer, 2) == 0
        self.is_p = jnp.logical_not(self.is_q)
        self.segment = self.t - core + self.layer

    def near(self, d):
        layer = lax.rem(self.layer + d, self.plan.half)
        return jnp.where(self.forward, layer, self.plan.panels - 1 - layer)

    def far(self, q):
        half = self.plan.half
        return jnp.where(self.forward, half + q, half - 1 - q)

    def part(self, mine):
        pairs = self.plan.half // 2
        first = jnp.where(self.is_q == mine, pairs, 0)
        return [block for i in range(pairs) for block in (self.near(first + i), self.far(first + i))]


def call(kernel, out_shapes, operands, scratch=(), out_space=pltpu.HBM, flops=1):
    return pl.pallas_call(
        kernel,
        out_shape=list(out_shapes),
        in_specs=[HBM] * len(operands),
        out_specs=[pl.BlockSpec(memory_space=out_space)] * len(out_shapes),
        scratch_shapes=list(scratch),
        compiler_params=pltpu.CompilerParams(vmem_limit_bytes=VMEM_BYTES),
        cost_estimate=pl.CostEstimate(flops=flops, bytes_accessed=1, transcendentals=0),
    )(*operands)


def bf16(*shape):
    return jax.ShapeDtypeStruct(shape, jnp.bfloat16)


def band(ref, block, rows):
    start = block * rows
    return ref.at[pl.ds(start if isinstance(block, int) else pl.multiple_of(start, rows), rows), :]


class Copies:
    def __init__(self, sems):
        self.sems, self.count = sems, 0

    def start(self, pairs, condition=None):
        copies = [pltpu.make_async_copy(a, b, self.sems.at[self.count + i]) for i, (a, b) in enumerate(pairs)]
        self.count += len(copies)
        self._start(copies, condition)
        return copies

    def start_either(self, condition, pairs, other_pairs):
        first = self.count
        copies = self.start(pairs, condition)
        self.count = first
        self.start(other_pairs, jnp.logical_not(condition))
        return copies

    @staticmethod
    def _start(copies, condition):
        def run():
            for copy in copies:
                copy.start()

        run() if condition is None else pl.when(condition)(run)


def wait(copies):
    for copy in copies:
        copy.wait()


def full_pairs(place, mine, theirs, target):
    rows = target.shape[0] // place.plan.panels
    return [
        (band(half, i, rows), band(target, block, rows))
        for half, is_mine in ((mine, True), (theirs, False))
        for i, block in enumerate(place.part(is_mine))
    ]


class Raw:
    def __init__(self, place, refs):
        half = place.plan.half
        self.place = place
        self.near = {True: refs[:half], False: refs[half : 2 * half]}
        self.far = {True: refs[2 * half : 3 * half], False: refs[3 * half : 4 * half]}

    @staticmethod
    def take(plan, refs):
        return refs[: 4 * plan.half], refs[4 * plan.half :]

    def start(self, copies, of_q, index, target, far_index=None, only_half=False):
        place, half = self.place, self.place.plan.half
        rows = self.near[True][0].shape[1]

        def pairs(mine):
            on_q = of_q == mine
            result = []
            ds = range(half // 2 if on_q else 0, half if on_q else half // 2) if only_half else range(half)
            for i, d in enumerate(ds):
                near, far = (2 * i, 2 * i + 1) if only_half else (place.near(d), place.far(d))
                result.append((self.near[mine][d].at[index], band(target, near, rows)))
                far_ref = self.far[mine][d] if far_index is None else self.far[mine][d].at[far_index]
                result.append((far_ref, band(target, far, rows)))
            return result

        return copies.start_either(place.is_q if of_q else place.is_p, pairs(True), pairs(False))


def product(out, a, b, finish=lambda acc, rows: acc, b_transposed=False, tile=TILE):
    n = out.shape[0]
    tile = min(tile, n)
    dims = (((1,), (1 if b_transposed else 0,)), ((), ()))

    @pl.loop(0, n // tile)
    def _(i):
        rows = pl.ds(pl.multiple_of(i * tile, tile), tile)
        acc = lax.dot_general(a[rows, :], b[...], dims, preferred_element_type=jnp.float32)
        out[rows, :] = finish(acc, rows).astype(jnp.bfloat16)


def upper_rows(place, out, a, b):
    rows = a.shape[0] // place.plan.panels
    for i, block in enumerate(place.part(True)):
        columns = pl.ds(pl.multiple_of(block * rows, rows), rows)
        acc = lax.dot_general(a[:, columns], b[...], (((0,), (0,)), ((), ())), preferred_element_type=jnp.float32)
        out[i * rows : (i + 1) * rows, :] = acc.astype(jnp.bfloat16)


def identity(rows, n):
    shape = (rows.size, n)
    row = lax.broadcasted_iota(jnp.int32, shape, 0) + rows.start
    return (row == lax.broadcasted_iota(jnp.int32, shape, 1)).astype(jnp.float32)


def iterates(n, cp, jq, u, x1, r):
    def first_iterate(acc, rows):
        x1[rows, :] = (identity(rows, n) - acc.astype(jnp.bfloat16)).astype(jnp.bfloat16)
        return acc

    product(u, cp, jq, first_iterate, tile=n)
    product(r, u, x1, lambda acc, rows: identity(rows, n) + u[rows, :] - acc, tile=n)


def plus(ref):
    return lambda acc, rows: acc + ref[rows, :]


def combine_front(place, copies, stride, loads, stored, cp, jq, aq, ah, ch, x1, r, full, u, f):
    load_cp, load_jq, load_ah, load_aq, load_ch = loads
    usable = place.segment >= stride
    wait(load_cp + load_jq)
    pl.when(usable)(lambda: iterates(cp.shape[0], cp, jq, full, x1, r))
    stores = copies.start(list(zip((x1, r), stored)))
    wait(load_ah)

    @pl.when(usable)
    def _():
        product(u, ah, x1)
        product(f, u, r)

    stores += copies.start([(f, stored[2])])
    pl.when(usable)(lambda: product(u, f, cp))
    wait(load_aq + load_ch)
    pl.when(usable)(lambda: product(ch, u, aq, plus(ch), b_transposed=True))
    return stores


def first_kernel(plan, stride, *refs):
    pairs = plan.half // 2
    raw, refs = Raw.take(plan, refs)
    kept, late, refs = refs[:pairs], refs[pairs : 2 * pairs], refs[2 * pairs :]
    c_ref, jq_ref, x1_ref, r_ref, f_ref, cp, jq, aq, ah, ch, x1, r, full, u, f, sems = refs
    place, copies = Place(plan), Copies(sems)
    raw_c = Raw(place, [*raw[: 2 * plan.half], *late, *late, *kept, *late])
    raw = Raw(place, raw)
    loads = [
        raw.start(copies, False, 0, cp, 0),
        raw.start(copies, True, 2, jq, 0),
        raw.start(copies, True, 1, ah, 1, only_half=True),
        raw.start(copies, True, 1, aq, 1),
        raw_c.start(copies, True, 0, ch, only_half=True),
    ]
    stored = (x1_ref, r_ref, f_ref)
    stores = combine_front(place, copies, stride, loads, stored, cp, jq, aq, ah, ch, x1, r, full, u, f)
    wait(stores + copies.start([(ch, c_ref), (jq, jq_ref)]))


def trans_info_kernel(plan, stride, f_ref, jq_ref, x1_ref, r_ref, *refs):
    raw_first, refs = Raw.take(plan, refs)
    raw_a, refs = Raw.take(plan, refs)
    raw_j, refs = Raw.take(plan, refs)
    a_ref, j_ref, f, ap, jq, x1, r, ah, u, w, jh, sems = refs
    place, copies = Place(plan), Copies(sems)
    raw_first, raw_a, raw_j = Raw(place, raw_first), Raw(place, raw_a), Raw(place, raw_j)
    usable = place.segment >= stride
    rows = ap.shape[0] // plan.panels
    load_ap = raw_a.start(copies, False, 1, ap)
    load_f = copies.start([(f_ref, f)])
    load_jq = copies.start([(jq_ref, jq)])
    load_x1 = copies.start([(x1_ref, x1)])
    load_r = copies.start([(r_ref, r)])
    load_jh = raw_j.start(copies, False, 2, jh, only_half=True)
    load_ah = raw_first.start(copies, True, 1, ah, 1, only_half=True)
    wait(load_ap + load_f + load_ah)
    pl.when(usable)(lambda: product(ah, f, ap))
    store_a = copies.start([(ah, a_ref)])
    wait(load_jq)
    pl.when(usable)(lambda: upper_rows(place, u, ap, jq))
    wait(load_x1)
    pl.when(usable)(lambda: product(w, u, x1))
    wait(load_r + load_jh)

    @pl.when(usable)
    def _():
        product(u, w, r)
        product(jh, u, ap, plus(jh))

    @pl.when(jnp.logical_not(usable))
    def _():
        for i, block in enumerate(place.part(True)):
            jh[i * rows : (i + 1) * rows, :] = jq[pl.ds(pl.multiple_of(block * rows, rows), rows), :]

    wait(copies.start([(jh, j_ref)]) + store_a)


def store_blocks(plan, copies, result, far, near):
    pairs = plan.half // 2
    rows = result.shape[0] // plan.half
    parts = len(far) // pairs
    stores = [
        (result.at[pl.ds((2 * (k % pairs) + 1) * rows + k // pairs * (rows // parts), rows // parts), :], piece)
        for k, piece in enumerate(far)
    ]
    stores += [(result.at[pl.ds(2 * i * rows, rows), :], piece) for i, piece in enumerate(near)]
    return copies.start(stores)


def front_kernel(plan, stride, c_mine, c_theirs, j_mine, j_theirs, a_mine, a_theirs, cq_mine, *refs):
    far, near = refs[: plan.half], refs[plan.half : plan.half + plan.half // 2]
    f_ref, x1_ref, r_ref, cp, jq, aq, ah, ch, x1, r, full, u, f, sems = refs[-14:]
    place, copies = Place(plan), Copies(sems)
    loads = [
        copies.start(full_pairs(place, c_mine, c_theirs, cp)),
        copies.start(full_pairs(place, j_mine, j_theirs, jq)),
        copies.start([(a_mine, ah)]),
        copies.start(full_pairs(place, a_mine, a_theirs, aq)),
        copies.start([(cq_mine, ch)]),
    ]
    stored = (x1_ref, r_ref, f_ref)
    stores = combine_front(place, copies, stride, loads, stored, cp, jq, aq, ah, ch, x1, r, full, u, f)
    wait(store_blocks(plan, copies, ch, far, near) + stores)


def trans_kernel(plan, stride, a_mine, a_theirs, f_ref, aq_mine, *refs):
    pairs = plan.half // 2
    c_near, far, near, refs = refs[:pairs], refs[pairs : 2 * pairs], refs[2 * pairs : 3 * pairs], refs[3 * pairs :]
    ap, f, ah, c, sems = refs
    place, copies = Place(plan), Copies(sems)
    rows = ah.shape[0] // plan.half
    usable = place.segment >= stride
    loads = copies.start([(f_ref, f), (aq_mine, ah)]) + copies.start(full_pairs(place, a_mine, a_theirs, ap))
    c_blocks = [c.at[pl.ds(i * rows, rows), :] for i in range(pairs)]
    load_c = copies.start(list(zip(c_near, c_blocks)))
    wait(loads)
    pl.when(usable)(lambda: product(ah, f, ap))
    stores = store_blocks(plan, copies, ah, far, [x.at[1] for x in near])
    wait(load_c)
    wait(copies.start([(block, x.at[0]) for block, x in zip(c_blocks, near)]) + stores)


def upper_kernel(plan, stride, a_mine, a_theirs, j_mine, j_theirs, x1_ref, r_ref, h_ref, ap, jq, x1, r, u, w, sems):
    place, copies = Place(plan), Copies(sems)

    @pl.when(place.segment >= stride)
    def _():
        load_ap = copies.start(full_pairs(place, a_mine, a_theirs, ap))
        load_jq = copies.start(full_pairs(place, j_mine, j_theirs, jq))
        load_x1 = copies.start([(x1_ref, x1)])
        load_r = copies.start([(r_ref, r)])
        wait(load_ap + load_jq)
        upper_rows(place, u, ap, jq)
        wait(load_x1)
        product(w, u, x1)
        wait(load_r)
        product(u, w, r)
        wait(copies.start([(u, h_ref)]))


def info_kernel(plan, stride, h_ref, a_mine, a_theirs, jp_mine, jq_mine, *refs):
    pairs = plan.half // 2
    far, near = refs[:pairs], refs[pairs : 2 * pairs]
    h, ap, jh, sems = refs[-4:]
    place, copies = Place(plan), Copies(sems)
    usable = place.segment >= stride
    load_jh = copies.start_either(usable, [(jp_mine, jh)], [(jq_mine, jh)])
    wait(load_jh + copies.start([(h_ref, h)]) + copies.start(full_pairs(place, a_mine, a_theirs, ap)))
    pl.when(usable)(lambda: product(jh, h, ap, plus(jh)))
    wait(store_blocks(plan, copies, jh, far, near))


def home_kernel(plan, *refs):
    half, pairs = plan.half, plan.half // 2
    c_far, a_far, ca_near = refs[:half], refs[half : half + pairs], refs[half + pairs : 2 * half]
    j_far, j_near = refs[2 * half : 2 * half + pairs], refs[2 * half + pairs : 3 * half]
    f_out, b_out, sems = refs[3 * half :]
    rows = f_out.shape[1]
    t, z = lax.axis_index("tm"), lax.axis_index("panel")
    waits = []
    places = [(f_out, t, z), (b_out, plan.groups - 1 - t, plan.panels - 1 - z)]
    for out, segment, panel in places:
        distance = lax.rem(panel + half - lax.rem(segment, 2), half)
        which = jnp.where(panel >= half, lax.rem(panel, pairs), pairs + lax.rem(distance, pairs))
        first = len(waits)
        for i in range(pairs):
            halves = [out.at[0, pl.ds(k * (rows // 2), rows // 2), :] for k in range(2)]
            far = [(c_far[i], halves[0]), (c_far[pairs + i], halves[1]), (a_far[i], out.at[1]), (j_far[i], out.at[2])]
            near = [(ca_near[i].at[k], out.at[k]) for k in range(2)] + [(j_near[i], out.at[2])]
            for owner, moves in ((i, far), (pairs + i, near)):
                @pl.when(which == owner)
                def _():
                    for k, (source_ref, target) in enumerate(moves):
                        at = k - 1 if len(moves) == 4 and k > 0 else k
                        pltpu.make_async_copy(source_ref, target, sems.at[first + at]).start()
        for matrix in range(3):
            waits.append(pltpu.make_async_copy(j_far[0], out.at[matrix], sems.at[first + matrix]))
    wait(waits)


def after(x, *others):
    return lax.optimization_barrier((x, *others))[0]


def shards(plan, forward_element, backward_element):
    forward, backward = forward_element[:, 0], backward_element[:, 0]
    rows, n = forward.shape[1:]
    half = plan.half
    full, part, block = bf16(n, n), bf16(n // 2, n), bf16(rows, n)
    square, slab = pltpu.VMEM((n, n), jnp.bfloat16), pltpu.VMEM((n // 2, n), jnp.bfloat16)
    sems = pltpu.SemaphoreType.DMA((12 * half,))

    def send(x, routes):
        return lax.ppermute(x, AXES, routes)

    def swap(x):
        return send(x, plan.core)

    def kernel(body, outs, operands, scratch, **options):
        return call(functools.partial(body, plan, *options.pop("static", ())), outs, operands, [*scratch, sems], **options)

    t, z = lax.axis_index("tm"), lax.axis_index("panel")
    layer = jnp.where(z < half, z, plan.panels - 1 - z)
    core = jnp.where(z < half, t, plan.groups - 1 - t) % 2
    is_q, special = (core + layer) % 2 == 0, (core == 1) & (layer == 0)
    other_c = jnp.where(z < half, backward[0], forward[0])
    other_ja = jnp.stack([jnp.where(z < half, backward[i], forward[i]) for i in (2, 1)])
    forward, backward, _ = lax.optimization_barrier((forward, backward, other_ja))
    own = jnp.where(z < half, forward, backward)

    far_c = [send(other_c, route) for route in plan.cross]
    far_ja = [send(other_ja, route) for route in plan.cross]
    local = [send(own, plan.gather[d]) for d in range(1, half)]
    onward_local = send(after(own, *far_c), plan.onward)
    far_c_of_p = [send(x, plan.forward) for x in far_c]
    far_first = [jnp.where(is_q, q, p[None]) for q, p in zip(far_ja, far_c_of_p)]
    first_swap = [swap(x) for x in far_first]
    near = [jnp.where(special, onward_local, own), *local]
    near_swap = [swap(x) for x in near]
    nears = [*near, *near_swap]
    raw_first = [*nears, *far_first, *first_swap]
    kept_c = [swap(x) for x in far_c[: half // 2]]

    rest = [send(after(x, *far_c_of_p), plan.forward) for x in far_ja]

    c_new, jq, x1, r, f = kernel(
        first_kernel,
        [part, full, full, full, part],
        [*raw_first, *kept_c, *far_c[half // 2 :]],
        [square] * 3 + [slab] * 2 + [square] * 3 + [slab] * 2,
        static=(1,),
    )
    rest = [after(x, c_new) for x in rest]
    j_rest, a_rest = [x[0] for x in rest], [x[1] for x in rest]
    raw_rest = [*nears, *a_rest, *[swap(x) for x in a_rest], *nears, *j_rest, *[swap(x) for x in j_rest]]
    a_new, j_new = kernel(
        trans_info_kernel,
        [part] * 2,
        [after(f, c_new), jq, x1, r, *raw_first, *raw_rest],
        [slab] + [square] * 4 + [slab] * 4,
        static=(1,),
    )
    j_swap, a_swap = swap(j_new), swap(a_new)
    c_next = send(c_new, plan.next)
    c_next, a_new = lax.optimization_barrier((c_next, a_new))
    c_next_swap = swap(c_next)
    a_next = send(a_new, plan.next)

    pairs = range(half // 2)
    blocks = [block for _ in pairs]
    far, near = [plan.home[True, i] for i in pairs], [plan.home[False, i] for i in pairs]

    def send_home(pieces, routes):
        return [send(x, route) for x, route in zip(pieces, routes)]

    *c_pieces, f, x1, r = kernel(
        front_kernel,
        [*[bf16(rows // 2, n)] * half, *blocks, part, full, full],
        [c_next, c_next_swap, j_new, j_swap, a_new, a_swap, c_new],
        [square] * 3 + [slab] * 2 + [square] * 3 + [slab] * 2,
        static=(2,),
    )
    c_far, c_near = send_home(c_pieces[:half], far * 2), c_pieces[half:]
    j_next = send(after(j_new, a_next), plan.next)
    a_next = after(a_next, f, *c_far[: half // 2])
    a_next_swap = swap(a_next)
    a_pieces = kernel(
        trans_kernel,
        [*blocks, *[bf16(2, rows, n) for _ in pairs]],
        [a_next, after(a_next_swap, *c_far), f, a_new, *c_near],
        [square] + [slab] * 3,
        static=(2,),
    )
    a_far = send_home(a_pieces[: half // 2], far)
    ca_near = send_home(a_pieces[half // 2 :], near)
    (h,) = kernel(
        upper_kernel,
        [part],
        [a_next, a_next_swap, j_new, j_swap, after(x1, *a_pieces), r],
        [square] * 4 + [slab] * 2,
        static=(2,),
    )
    j_pieces = kernel(
        info_kernel,
        [*blocks, *blocks],
        [h, a_next, a_next_swap, after(j_next, h), j_new],
        [slab, square, slab],
        static=(2,),
    )
    j_home = send_home([after(x, *a_far, *ca_near) for x in j_pieces], [*far, *near])

    f_out, b_out = kernel(
        home_kernel,
        [bf16(3, rows, n)] * 2,
        [*c_far, *a_far, *ca_near, *j_home],
        [],
        out_space=pltpu.VMEM,
    )
    return f_out[:, None], b_out[:, None]


def solution(mesh):
    plan = Plan(mesh.shape["tm"], mesh.shape["panel"])
    spec = P(None, "tm", "panel", None)
    return jax.shard_map(
        functools.partial(shards, plan),
        mesh=mesh,
        in_specs=(spec, spec),
        out_specs=(spec, spec),
        check_vma=False,
    )
```

```python
import functools

import jax
import jax.numpy as jnp
from jax import lax
from jax.experimental import pallas as pl
from jax.experimental.pallas import tpu as pltpu
from jax.sharding import PartitionSpec as P

AXES = ("tm", "panel")
VMEM_BYTES = 32 * 2**20
TILE = 512
HBM = pl.BlockSpec(memory_space=pltpu.HBM)


class Plan:
    def __init__(self, groups, panels):
        self.groups, self.panels, self.half = groups, panels, panels // 2
        assert groups % 2 == 0 and panels % 4 == 0
        columns = range(groups // 2)
        half = self.half

        def table(forward_routes):
            last = groups * panels - 1
            routes = [(a * panels + b, c * panels + d) for (a, b), (c, d) in forward_routes]
            return routes + [(last - source, last - target) for source, target in routes]

        def in_range(routes):
            return [route for route in routes if route[1][0] < groups]

        everyone = [(t, z) for t in range(groups) for z in range(panels)]
        self.core = [(t * panels + z, (t ^ 1) * panels + z) for t, z in everyone]
        q_of = {t: (t, t % 2) for t in range(groups)}
        p_of = {t: (t, 1) if t % 2 == 0 else (t + 2, 0) for t in range(groups)}
        self.cross = [table([((t, half + q), q_of[t]) for t in range(groups)]) for q in range(half)]
        self.forward = table(in_range([(q_of[t], p_of[t]) for t in range(groups)]))
        self.gather = {}
        for d in range(1, half):
            routes = [((t, (q_of[t][1] + d) % half), q_of[t]) for t in range(groups)]
            routes += [((t, (p_of[t][1] + d) % half), p_of[t]) for t in range(groups)]
            self.gather[d] = table(in_range(routes))
        self.onward = table(in_range([((t, 0), p_of[t]) for t in range(1, groups, 2)]))
        active = [(2 * c + core, layer) for c in columns for core in (0, 1) for layer in (0, 1)]
        self.next = table(in_range([((t, z), (t + 2, z)) for t, z in active]))
        self.home = {}
        for far in (True, False):
            for i in range(half // 2):
                routes = []
                for t, z in active:
                    d = i + (half // 2 if (t + z) % 2 == 0 else 0)
                    routes.append(((t, z), (t - t % 2 + z, half + d if far else (z + d) % half)))
                self.home[far, i] = table(routes)


class Place:
    def __init__(self, plan):
        t, z = lax.axis_index("tm"), lax.axis_index("panel")
        self.plan = plan
        self.forward = z < plan.half
        self.layer = jnp.where(self.forward, z, plan.panels - 1 - z)
        self.t = jnp.where(self.forward, t, plan.groups - 1 - t)
        core = lax.rem(self.t, 2)
        self.is_q = lax.rem(core + self.layer, 2) == 0
        self.is_p = jnp.logical_not(self.is_q)
        self.segment = self.t - core + self.layer

    def near(self, d):
        layer = lax.rem(self.layer + d, self.plan.half)
        return jnp.where(self.forward, layer, self.plan.panels - 1 - layer)

    def far(self, q):
        half = self.plan.half
        return jnp.where(self.forward, half + q, half - 1 - q)

    def part(self, mine):
        pairs = self.plan.half // 2
        first = jnp.where(self.is_q == mine, pairs, 0)
        return [block for i in range(pairs) for block in (self.near(first + i), self.far(first + i))]


def call(kernel, out_shapes, operands, scratch=(), flops=1, aliases=None):
    return pl.pallas_call(
        kernel,
        out_shape=list(out_shapes),
        in_specs=[HBM] * len(operands),
        out_specs=[HBM] * len(out_shapes),
        input_output_aliases=aliases or {},
        scratch_shapes=list(scratch),
        compiler_params=pltpu.CompilerParams(vmem_limit_bytes=VMEM_BYTES),
        cost_estimate=pl.CostEstimate(flops=flops, bytes_accessed=1, transcendentals=0),
    )(*operands)


def bf16(*shape):
    return jax.ShapeDtypeStruct(shape, jnp.bfloat16)


def band(ref, block, rows):
    start = block * rows
    return ref.at[pl.ds(start if isinstance(block, int) else pl.multiple_of(start, rows), rows), :]


class Copies:
    def __init__(self, sems):
        self.sems, self.count = sems, 0

    def start(self, pairs, condition=None):
        copies = [pltpu.make_async_copy(a, b, self.sems.at[self.count + i]) for i, (a, b) in enumerate(pairs)]
        self.count += len(copies)
        self._start(copies, condition)
        return copies

    def start_either(self, condition, pairs, other_pairs):
        first = self.count
        copies = self.start(pairs, condition)
        self.count = first
        self.start(other_pairs, jnp.logical_not(condition))
        return copies

    @staticmethod
    def _start(copies, condition):
        def run():
            for copy in copies:
                copy.start()

        run() if condition is None else pl.when(condition)(run)


def wait(copies):
    for copy in copies:
        copy.wait()


def full_pairs(place, mine, theirs, target):
    rows = target.shape[0] // place.plan.panels
    return [
        (band(half, i, rows), band(target, block, rows))
        for half, is_mine in ((mine, True), (theirs, False))
        for i, block in enumerate(place.part(is_mine))
    ]


class Raw:
    def __init__(self, place, refs):
        half = place.plan.half
        self.place = place
        self.near = {True: refs[:half], False: refs[half : 2 * half]}
        self.far = {True: refs[2 * half : 3 * half], False: refs[3 * half : 4 * half]}

    @staticmethod
    def take(plan, refs):
        return refs[: 4 * plan.half], refs[4 * plan.half :]

    def start(self, copies, of_q, index, target, far_index=None, only_half=False):
        place, half = self.place, self.place.plan.half
        rows = self.near[True][0].shape[1]

        def pairs(mine):
            on_q = of_q == mine
            result = []
            ds = range(half // 2 if on_q else 0, half if on_q else half // 2) if only_half else range(half)
            for i, d in enumerate(ds):
                near, far = (2 * i, 2 * i + 1) if only_half else (place.near(d), place.far(d))
                result.append((self.near[mine][d].at[index], band(target, near, rows)))
                far_ref = self.far[mine][d] if far_index is None else self.far[mine][d].at[far_index]
                result.append((far_ref, band(target, far, rows)))
            return result

        return copies.start_either(place.is_q if of_q else place.is_p, pairs(True), pairs(False))


def product(out, a, b, finish=lambda acc, rows: acc, b_transposed=False, tile=TILE):
    n = out.shape[0]
    tile = min(tile, n)
    dims = (((1,), (1 if b_transposed else 0,)), ((), ()))

    @pl.loop(0, n // tile)
    def _(i):
        rows = pl.ds(pl.multiple_of(i * tile, tile), tile)
        acc = lax.dot_general(a[rows, :], b[...], dims, preferred_element_type=jnp.float32)
        out[rows, :] = finish(acc, rows).astype(jnp.bfloat16)


def upper_rows(place, out, a, b):
    rows = a.shape[0] // place.plan.panels
    for i, block in enumerate(place.part(True)):
        columns = pl.ds(pl.multiple_of(block * rows, rows), rows)
        acc = lax.dot_general(a[:, columns], b[...], (((0,), (0,)), ((), ())), preferred_element_type=jnp.float32)
        out[i * rows : (i + 1) * rows, :] = acc.astype(jnp.bfloat16)


def identity(rows, n):
    shape = (rows.size, n)
    row = lax.broadcasted_iota(jnp.int32, shape, 0) + rows.start
    return (row == lax.broadcasted_iota(jnp.int32, shape, 1)).astype(jnp.float32)


def iterates(n, cp, jq, u, x1, r):
    def first_iterate(acc, rows):
        x1[rows, :] = (identity(rows, n) - acc.astype(jnp.bfloat16)).astype(jnp.bfloat16)
        return acc

    product(u, cp, jq, first_iterate, tile=n)
    product(r, u, x1, lambda acc, rows: identity(rows, n) + u[rows, :] - acc, tile=n)


def plus(ref):
    return lambda acc, rows: acc + ref[rows, :]


def combine_front(place, copies, stride, loads, stored, cp, jq, aq, ah, ch, x1, r, full, u, f):
    load_cp, load_jq, load_ah, load_aq, load_ch = loads
    usable = place.segment >= stride
    wait(load_cp + load_jq)
    pl.when(usable)(lambda: iterates(cp.shape[0], cp, jq, full, x1, r))
    stores = copies.start(list(zip((x1, r), stored)))
    wait(load_ah)

    @pl.when(usable)
    def _():
        product(u, ah, x1)
        product(f, u, r)

    stores += copies.start([(f, stored[2])])
    pl.when(usable)(lambda: product(u, f, cp))
    wait(load_aq + load_ch)
    pl.when(usable)(lambda: product(ch, u, aq, plus(ch), b_transposed=True))
    return stores


def first_kernel(plan, stride, *refs):
    pairs = plan.half // 2
    raw, refs = Raw.take(plan, refs)
    kept, late, refs = refs[:pairs], refs[pairs : 2 * pairs], refs[2 * pairs :]
    c_ref, jq_ref, x1_ref, r_ref, f_ref, cp, jq, aq, ah, ch, x1, r, full, u, f, sems = refs
    place, copies = Place(plan), Copies(sems)
    raw_c = Raw(place, [*raw[: 2 * plan.half], *late, *late, *kept, *late])
    raw = Raw(place, raw)
    loads = [
        raw.start(copies, False, 0, cp, 0),
        raw.start(copies, True, 2, jq, 0),
        raw.start(copies, True, 1, ah, 1, only_half=True),
        raw.start(copies, True, 1, aq, 1),
        raw_c.start(copies, True, 0, ch, only_half=True),
    ]
    stored = (x1_ref, r_ref, f_ref)
    stores = combine_front(place, copies, stride, loads, stored, cp, jq, aq, ah, ch, x1, r, full, u, f)
    wait(stores + copies.start([(ch, c_ref), (jq, jq_ref)]))


def trans_info_kernel(plan, stride, f_ref, jq_ref, x1_ref, r_ref, *refs):
    raw_first, refs = Raw.take(plan, refs)
    raw_a, refs = Raw.take(plan, refs)
    raw_j, refs = Raw.take(plan, refs)
    a_ref, j_ref, f, ap, jq, x1, r, ah, u, w, jh, sems = refs
    place, copies = Place(plan), Copies(sems)
    raw_first, raw_a, raw_j = Raw(place, raw_first), Raw(place, raw_a), Raw(place, raw_j)
    usable = place.segment >= stride
    rows = ap.shape[0] // plan.panels
    load_ap = raw_a.start(copies, False, 1, ap)
    load_f = copies.start([(f_ref, f)])
    load_jq = copies.start([(jq_ref, jq)])
    load_x1 = copies.start([(x1_ref, x1)])
    load_r = copies.start([(r_ref, r)])
    load_jh = raw_j.start(copies, False, 2, jh, only_half=True)
    load_ah = raw_first.start(copies, True, 1, ah, 1, only_half=True)
    wait(load_ap + load_f + load_ah)
    pl.when(usable)(lambda: product(ah, f, ap))
    store_a = copies.start([(ah, a_ref)])
    wait(load_jq)
    pl.when(usable)(lambda: upper_rows(place, u, ap, jq))
    wait(load_x1)
    pl.when(usable)(lambda: product(w, u, x1))
    wait(load_r + load_jh)

    @pl.when(usable)
    def _():
        product(u, w, r)
        product(jh, u, ap, plus(jh))

    @pl.when(jnp.logical_not(usable))
    def _():
        for i, block in enumerate(place.part(True)):
            jh[i * rows : (i + 1) * rows, :] = jq[pl.ds(pl.multiple_of(block * rows, rows), rows), :]

    wait(copies.start([(jh, j_ref)]) + store_a)


def store_blocks(plan, copies, result, far, near):
    pairs = plan.half // 2
    rows = result.shape[0] // plan.half
    parts = len(far) // pairs
    stores = [
        (result.at[pl.ds((2 * (k % pairs) + 1) * rows + k // pairs * (rows // parts), rows // parts), :], piece)
        for k, piece in enumerate(far)
    ]
    stores += [(result.at[pl.ds(2 * i * rows, rows), :], piece) for i, piece in enumerate(near)]
    return copies.start(stores)


def front_kernel(plan, stride, c_mine, c_theirs, j_mine, j_theirs, a_mine, a_theirs, cq_mine, *refs):
    far, near = refs[: plan.half], refs[plan.half : plan.half + plan.half // 2]
    f_ref, x1_ref, r_ref, cp, jq, aq, ah, ch, x1, r, full, u, f, sems = refs[-14:]
    place, copies = Place(plan), Copies(sems)
    loads = [
        copies.start(full_pairs(place, c_mine, c_theirs, cp)),
        copies.start(full_pairs(place, j_mine, j_theirs, jq)),
        copies.start([(a_mine, ah)]),
        copies.start(full_pairs(place, a_mine, a_theirs, aq)),
        copies.start([(cq_mine, ch)]),
    ]
    stored = (x1_ref, r_ref, f_ref)
    stores = combine_front(place, copies, stride, loads, stored, cp, jq, aq, ah, ch, x1, r, full, u, f)
    wait(store_blocks(plan, copies, ch, far, near) + stores)


def trans_kernel(plan, stride, a_mine, a_theirs, f_ref, aq_mine, *refs):
    pairs = plan.half // 2
    c_near, far, near, refs = refs[:pairs], refs[pairs : 2 * pairs], refs[2 * pairs : 3 * pairs], refs[3 * pairs :]
    ap, f, ah, c, sems = refs
    place, copies = Place(plan), Copies(sems)
    rows = ah.shape[0] // plan.half
    usable = place.segment >= stride
    loads = copies.start([(f_ref, f), (aq_mine, ah)]) + copies.start(full_pairs(place, a_mine, a_theirs, ap))
    c_blocks = [c.at[pl.ds(i * rows, rows), :] for i in range(pairs)]
    load_c = copies.start(list(zip(c_near, c_blocks)))
    wait(loads)
    pl.when(usable)(lambda: product(ah, f, ap))
    stores = store_blocks(plan, copies, ah, far, [x.at[1] for x in near])
    wait(load_c)
    wait(copies.start([(block, x.at[0]) for block, x in zip(c_blocks, near)]) + stores)


def upper_kernel(plan, stride, a_mine, a_theirs, j_mine, j_theirs, x1_ref, r_ref, h_ref, ap, jq, x1, r, u, w, sems):
    place, copies = Place(plan), Copies(sems)

    @pl.when(place.segment >= stride)
    def _():
        load_ap = copies.start(full_pairs(place, a_mine, a_theirs, ap))
        load_jq = copies.start(full_pairs(place, j_mine, j_theirs, jq))
        load_x1 = copies.start([(x1_ref, x1)])
        load_r = copies.start([(r_ref, r)])
        wait(load_ap + load_jq)
        upper_rows(place, u, ap, jq)
        wait(load_x1)
        product(w, u, x1)
        wait(load_r)
        product(u, w, r)
        wait(copies.start([(u, h_ref)]))


def info_kernel(plan, stride, h_ref, a_mine, a_theirs, jp_mine, jq_mine, *refs):
    pairs = plan.half // 2
    far, near = refs[:pairs], refs[pairs : 2 * pairs]
    h, ap, jh, sems = refs[-4:]
    place, copies = Place(plan), Copies(sems)
    usable = place.segment >= stride
    load_jh = copies.start_either(usable, [(jp_mine, jh)], [(jq_mine, jh)])
    wait(load_jh + copies.start([(h_ref, h)]) + copies.start(full_pairs(place, a_mine, a_theirs, ap)))
    pl.when(usable)(lambda: product(jh, h, ap, plus(jh)))
    wait(store_blocks(plan, copies, jh, far, near))


def home_blocks(plan, rows):
    half, pairs = plan.half, plan.half // 2
    t, z = lax.axis_index("tm"), lax.axis_index("panel")
    tests = []
    for segment, panel in ((t, z), (plan.groups - 1 - t, plan.panels - 1 - z)):
        distance = lax.rem(panel + half - lax.rem(segment, 2), half)
        which = jnp.where(panel >= half, lax.rem(panel, pairs), pairs + lax.rem(distance, pairs))
        tests.append(which)
    return tests


def home_kernel(plan, *refs):
    half, pairs = plan.half, plan.half // 2
    c_far, a_far, ca_near = refs[:half], refs[half : half + pairs], refs[half + pairs : 2 * half]
    outs, (held, sems) = refs[2 * half : 2 * half + 2], refs[2 * half + 2 :]
    rows = held.shape[2]
    part = rows // 2
    waits = []
    for k, which in enumerate(home_blocks(plan, rows)):
        c, a = held.at[k, 0], held.at[k, 1]
        for i in range(pairs):
            far = [(c_far[i], c.at[pl.ds(0, part), :], 0), (c_far[pairs + i], c.at[pl.ds(part, part), :], 0), (a_far[i], a, 1)]
            near = [(ca_near[i].at[0], c, 0), (ca_near[i].at[1], a, 1)]
            for owner, moves in ((i, far), (pairs + i, near)):
                for source, target, matrix in moves:
                    pl.when(which == owner)(pltpu.make_async_copy(source, target, sems.at[2 * k + matrix]).start)
        for matrix in range(2):
            waits.append(pltpu.make_async_copy(a_far[0], held.at[k, matrix], sems.at[2 * k + matrix]))
    wait(waits)
    run = [pltpu.make_async_copy(held.at[k], outs[k].at[pl.ds(0, 2)], sems.at[k]) for k in range(2)]
    for copy in run:
        copy.start()
    wait(run)


def home_info_kernel(plan, f_in, b_in, *refs):
    pairs = plan.half // 2
    j_far, j_near, outs, (held, sems) = refs[:pairs], refs[pairs : 2 * pairs], refs[2 * pairs : 2 * pairs + 2], refs[-2:]
    waits, run = [], []
    for k, which in enumerate(home_blocks(plan, held.shape[1])):
        for owner, source in enumerate([*j_far, *j_near]):
            pl.when(which == owner)(pltpu.make_async_copy(source, held.at[k], sems.at[k]).start)
        waits.append(pltpu.make_async_copy(j_far[0], held.at[k], sems.at[k]))
        run.append(pltpu.make_async_copy(held.at[k], outs[k].at[2], sems.at[2 + k]))
    for copy, store in zip(waits, run):
        copy.wait()
        store.start()
    wait(run)


def after(x, *others):
    return lax.optimization_barrier((x, *others))[0]


def shards(plan, forward_element, backward_element):
    forward, backward = forward_element[:, 0], backward_element[:, 0]
    rows, n = forward.shape[1:]
    half = plan.half
    full, part, block = bf16(n, n), bf16(n // 2, n), bf16(rows, n)
    square, slab = pltpu.VMEM((n, n), jnp.bfloat16), pltpu.VMEM((n // 2, n), jnp.bfloat16)
    sems = pltpu.SemaphoreType.DMA((12 * half,))

    def send(x, routes):
        return lax.ppermute(x, AXES, routes)

    def swap(x):
        return send(x, plan.core)

    def kernel(body, outs, operands, scratch, **options):
        return call(functools.partial(body, plan, *options.pop("static", ())), outs, operands, [*scratch, sems], **options)

    t, z = lax.axis_index("tm"), lax.axis_index("panel")
    layer = jnp.where(z < half, z, plan.panels - 1 - z)
    core = jnp.where(z < half, t, plan.groups - 1 - t) % 2
    is_q, special = (core + layer) % 2 == 0, (core == 1) & (layer == 0)
    other_c = jnp.where(z < half, backward[0], forward[0])
    other_ja = jnp.stack([jnp.where(z < half, backward[i], forward[i]) for i in (2, 1)])
    own = jnp.where(z < half, forward, backward)

    far_c = [send(other_c, route) for route in plan.cross]
    far_ja = [send(other_ja, route) for route in plan.cross]
    local = [send(own, plan.gather[d]) for d in range(1, half)]
    onward_local = send(after(own, *far_c), plan.onward)
    far_c_of_p = [send(x, plan.forward) for x in far_c]
    far_first = [jnp.where(is_q, q, p[None]) for q, p in zip(far_ja, far_c_of_p)]
    first_swap = [swap(x) for x in far_first]
    near = [jnp.where(special, onward_local, own), *local]
    near_swap = [swap(x) for x in near]
    nears = [*near, *near_swap]
    raw_first = [*nears, *far_first, *first_swap]
    kept_c = [swap(x) for x in far_c[: half // 2]]

    rest = [send(x, plan.forward) for x in far_ja]

    c_new, jq, x1, r, f = kernel(
        first_kernel,
        [part, full, full, full, part],
        [*raw_first, *kept_c, *far_c[half // 2 :]],
        [square] * 3 + [slab] * 2 + [square] * 3 + [slab] * 2,
        static=(1,),
    )
    rest = [after(x, c_new) for x in rest]
    j_rest, a_rest = [x[0] for x in rest], [x[1] for x in rest]
    raw_rest = [*nears, *a_rest, *[swap(x) for x in a_rest], *nears, *j_rest, *[swap(x) for x in j_rest]]
    a_new, j_new = kernel(
        trans_info_kernel,
        [part] * 2,
        [after(f, c_new), jq, x1, r, *raw_first, *raw_rest],
        [slab] + [square] * 4 + [slab] * 4,
        static=(1,),
    )
    j_swap, a_swap = swap(j_new), swap(a_new)
    c_next = send(c_new, plan.next)
    c_next, a_new = lax.optimization_barrier((c_next, a_new))
    c_next_swap = swap(c_next)
    a_next = send(a_new, plan.next)

    pairs = range(half // 2)
    blocks = [block for _ in pairs]
    far, near = [plan.home[True, i] for i in pairs], [plan.home[False, i] for i in pairs]

    def send_home(pieces, routes):
        return [send(x, route) for x, route in zip(pieces, routes)]

    *c_pieces, f, x1, r = kernel(
        front_kernel,
        [*[bf16(rows // 2, n)] * half, *blocks, part, full, full],
        [c_next, c_next_swap, j_new, j_swap, a_new, a_swap, c_new],
        [square] * 3 + [slab] * 2 + [square] * 3 + [slab] * 2,
        static=(2,),
    )
    c_far, c_near = send_home(c_pieces[:half], far * 2), c_pieces[half:]
    j_next = send(after(j_new, a_next), plan.next)
    a_next = after(a_next, f, *c_far[: half // 2])
    a_next_swap = swap(a_next)
    a_pieces = kernel(
        trans_kernel,
        [*blocks, *[bf16(2, rows, n) for _ in pairs]],
        [a_next, after(a_next_swap, *c_far), f, a_new, *c_near],
        [square] + [slab] * 3,
        static=(2,),
    )
    a_far = send_home(a_pieces[: half // 2], far)
    ca_near = send_home(a_pieces[half // 2 :], near)
    (h,) = kernel(
        upper_kernel,
        [part],
        [a_next, a_next_swap, j_new, j_swap, after(x1, *a_pieces), r],
        [square] * 4 + [slab] * 2,
        static=(2,),
    )
    j_pieces = kernel(
        info_kernel,
        [*blocks, *blocks],
        [h, a_next, a_next_swap, after(j_next, h), j_new],
        [slab, square, slab],
        static=(2,),
    )
    j_home = send_home([after(x, *a_far, *ca_near) for x in j_pieces], [*far, *near])

    outs = [bf16(3, rows, n)] * 2
    f_out, b_out = kernel(
        home_kernel,
        outs,
        [*c_far, *a_far, *ca_near],
        [pltpu.VMEM((2, 2, rows, n), jnp.bfloat16)],
        flops=n**3,
    )
    f_out, b_out = kernel(
        home_info_kernel,
        outs,
        [f_out, b_out, *j_home],
        [pltpu.VMEM((2, rows, n), jnp.bfloat16)],
        aliases={0: 0, 1: 1},
    )
    return f_out[:, None], b_out[:, None]


def solution(mesh):
    plan = Plan(mesh.shape["tm"], mesh.shape["panel"])
    spec = P(None, "tm", "panel", None)
    return jax.shard_map(
        functools.partial(shards, plan),
        mesh=mesh,
        in_specs=(spec, spec),
        out_specs=(spec, spec),
        check_vma=False,
    )
```

```python
import functools

import jax
import jax.numpy as jnp
from jax import lax
from jax.experimental import pallas as pl
from jax.experimental.pallas import tpu as pltpu
from jax.sharding import PartitionSpec as P

AXES = ("tm", "panel")
VMEM_BYTES = 32 * 2**20
TILE = 512
HBM = pl.BlockSpec(memory_space=pltpu.HBM)


class Plan:
    def __init__(self, groups, panels):
        self.groups, self.panels, self.half = groups, panels, panels // 2
        assert groups % 2 == 0 and panels % 4 == 0
        columns = range(groups // 2)
        half = self.half

        def table(forward_routes):
            last = groups * panels - 1
            routes = [(a * panels + b, c * panels + d) for (a, b), (c, d) in forward_routes]
            return routes + [(last - source, last - target) for source, target in routes]

        def in_range(routes):
            return [route for route in routes if route[1][0] < groups]

        everyone = [(t, z) for t in range(groups) for z in range(panels)]
        self.core = [(t * panels + z, (t ^ 1) * panels + z) for t, z in everyone]
        q_of = {t: (t, t % 2) for t in range(groups)}
        p_of = {t: (t, 1) if t % 2 == 0 else (t + 2, 0) for t in range(groups)}
        self.cross = [table([((t, half + q), q_of[t]) for t in range(groups)]) for q in range(half)]
        self.forward = table(in_range([(q_of[t], p_of[t]) for t in range(groups)]))
        self.gather = {}
        for d in range(1, half):
            routes = [((t, (q_of[t][1] + d) % half), q_of[t]) for t in range(groups)]
            routes += [((t, (p_of[t][1] + d) % half), p_of[t]) for t in range(groups)]
            self.gather[d] = table(in_range(routes))
        self.onward = table(in_range([((t, 0), p_of[t]) for t in range(1, groups, 2)]))
        active = [(2 * c + core, layer) for c in columns for core in (0, 1) for layer in (0, 1)]
        self.next = table(in_range([((t, z), (t + 2, z)) for t, z in active]))
        self.home = {}
        for far in (True, False):
            for i in range(half // 2):
                routes = []
                for t, z in active:
                    d = i + (half // 2 if (t + z) % 2 == 0 else 0)
                    routes.append(((t, z), (t - t % 2 + z, half + d if far else (z + d) % half)))
                self.home[far, i] = table(routes)


class Place:
    def __init__(self, plan):
        t, z = lax.axis_index("tm"), lax.axis_index("panel")
        self.plan = plan
        self.forward = z < plan.half
        self.layer = jnp.where(self.forward, z, plan.panels - 1 - z)
        self.t = jnp.where(self.forward, t, plan.groups - 1 - t)
        core = lax.rem(self.t, 2)
        self.is_q = lax.rem(core + self.layer, 2) == 0
        self.is_p = jnp.logical_not(self.is_q)
        self.segment = self.t - core + self.layer

    def near(self, d):
        layer = lax.rem(self.layer + d, self.plan.half)
        return jnp.where(self.forward, layer, self.plan.panels - 1 - layer)

    def far(self, q):
        half = self.plan.half
        return jnp.where(self.forward, half + q, half - 1 - q)

    def part(self, mine):
        pairs = self.plan.half // 2
        first = jnp.where(self.is_q == mine, pairs, 0)
        return [block for i in range(pairs) for block in (self.near(first + i), self.far(first + i))]


def call(kernel, out_shapes, operands, scratch=(), flops=1, aliases=None):
    return pl.pallas_call(
        kernel,
        out_shape=list(out_shapes),
        in_specs=[HBM] * len(operands),
        out_specs=[HBM] * len(out_shapes),
        input_output_aliases=aliases or {},
        scratch_shapes=list(scratch),
        compiler_params=pltpu.CompilerParams(vmem_limit_bytes=VMEM_BYTES),
        cost_estimate=pl.CostEstimate(flops=flops, bytes_accessed=1, transcendentals=0),
    )(*operands)


def bf16(*shape):
    return jax.ShapeDtypeStruct(shape, jnp.bfloat16)


def band(ref, block, rows):
    start = block * rows
    return ref.at[pl.ds(start if isinstance(block, int) else pl.multiple_of(start, rows), rows), :]


class Copies:
    def __init__(self, sems):
        self.sems, self.count = sems, 0

    def start(self, pairs, condition=None):
        copies = [pltpu.make_async_copy(a, b, self.sems.at[self.count + i]) for i, (a, b) in enumerate(pairs)]
        self.count += len(copies)
        self._start(copies, condition)
        return copies

    def start_either(self, condition, pairs, other_pairs):
        first = self.count
        copies = self.start(pairs, condition)
        self.count = first
        self.start(other_pairs, jnp.logical_not(condition))
        return copies

    @staticmethod
    def _start(copies, condition):
        def run():
            for copy in copies:
                copy.start()

        run() if condition is None else pl.when(condition)(run)


def wait(copies):
    for copy in copies:
        copy.wait()


def full_pairs(place, mine, theirs, target):
    rows = target.shape[0] // place.plan.panels
    return [
        (band(half, i, rows), band(target, block, rows))
        for half, is_mine in ((mine, True), (theirs, False))
        for i, block in enumerate(place.part(is_mine))
    ]


class Raw:
    def __init__(self, place, refs):
        half = place.plan.half
        self.place = place
        self.near = {True: refs[:half], False: refs[half : 2 * half]}
        self.far = {True: refs[2 * half : 3 * half], False: refs[3 * half : 4 * half]}

    @staticmethod
    def take(plan, refs):
        return refs[: 4 * plan.half], refs[4 * plan.half :]

    def start(self, copies, of_q, index, target, far_index=None, only_half=False):
        place, half = self.place, self.place.plan.half
        rows = self.near[True][0].shape[1]

        def pairs(mine):
            on_q = of_q == mine
            result = []
            ds = range(half // 2 if on_q else 0, half if on_q else half // 2) if only_half else range(half)
            for i, d in enumerate(ds):
                near, far = (2 * i, 2 * i + 1) if only_half else (place.near(d), place.far(d))
                result.append((self.near[mine][d].at[index], band(target, near, rows)))
                far_ref = self.far[mine][d] if far_index is None else self.far[mine][d].at[far_index]
                result.append((far_ref, band(target, far, rows)))
            return result

        return copies.start_either(place.is_q if of_q else place.is_p, pairs(True), pairs(False))


def product(out, a, b, finish=lambda acc, rows: acc, b_transposed=False, tile=TILE):
    n = out.shape[0]
    tile = min(tile, n)
    dims = (((1,), (1 if b_transposed else 0,)), ((), ()))

    @pl.loop(0, n // tile)
    def _(i):
        rows = pl.ds(pl.multiple_of(i * tile, tile), tile)
        acc = lax.dot_general(a[rows, :], b[...], dims, preferred_element_type=jnp.float32)
        out[rows, :] = finish(acc, rows).astype(jnp.bfloat16)


def upper_rows(place, out, a, b):
    rows = a.shape[0] // place.plan.panels
    for i, block in enumerate(place.part(True)):
        columns = pl.ds(pl.multiple_of(block * rows, rows), rows)
        acc = lax.dot_general(a[:, columns], b[...], (((0,), (0,)), ((), ())), preferred_element_type=jnp.float32)
        out[i * rows : (i + 1) * rows, :] = acc.astype(jnp.bfloat16)


def identity(rows, n):
    shape = (rows.size, n)
    row = lax.broadcasted_iota(jnp.int32, shape, 0) + rows.start
    return (row == lax.broadcasted_iota(jnp.int32, shape, 1)).astype(jnp.float32)


def iterates(n, cp, jq, u, x1, r):
    def first_iterate(acc, rows):
        x1[rows, :] = (identity(rows, n) - acc.astype(jnp.bfloat16)).astype(jnp.bfloat16)
        return acc

    product(u, cp, jq, first_iterate, tile=n)
    product(r, u, x1, lambda acc, rows: identity(rows, n) + u[rows, :] - acc, tile=n)


def plus(ref):
    return lambda acc, rows: acc + ref[rows, :]


def combine_front(place, copies, stride, loads, stored, cp, jq, aq, ah, ch, x1, r, full, u, f):
    load_cp, load_jq, load_ah, load_aq, load_ch = loads
    usable = place.segment >= stride
    wait(load_cp + load_jq)
    pl.when(usable)(lambda: iterates(cp.shape[0], cp, jq, full, x1, r))
    stores = copies.start(list(zip((x1, r), stored)))
    wait(load_ah)

    @pl.when(usable)
    def _():
        product(u, ah, x1)
        product(f, u, r)

    stores += copies.start([(f, stored[2])])
    pl.when(usable)(lambda: product(u, f, cp))
    wait(load_aq + load_ch)
    pl.when(usable)(lambda: product(ch, u, aq, plus(ch), b_transposed=True))
    return stores


def first_kernel(plan, stride, *refs):
    pairs = plan.half // 2
    raw, refs = Raw.take(plan, refs)
    kept, late, refs = refs[:pairs], refs[pairs : 2 * pairs], refs[2 * pairs :]
    c_ref, jq_ref, x1_ref, r_ref, f_ref, cp, jq, aq, ah, ch, x1, r, full, u, f, sems = refs
    place, copies = Place(plan), Copies(sems)
    raw_c = Raw(place, [*raw[: 2 * plan.half], *late, *late, *kept, *late])
    raw = Raw(place, raw)
    loads = [
        raw.start(copies, False, 0, cp, 0),
        raw.start(copies, True, 2, jq, 0),
        raw.start(copies, True, 1, ah, 1, only_half=True),
        raw.start(copies, True, 1, aq, 1),
        raw_c.start(copies, True, 0, ch, only_half=True),
    ]
    stored = (x1_ref, r_ref, f_ref)
    stores = combine_front(place, copies, stride, loads, stored, cp, jq, aq, ah, ch, x1, r, full, u, f)
    wait(stores + copies.start([(ch, c_ref), (jq, jq_ref)]))


def trans_info_kernel(plan, stride, f_ref, jq_ref, x1_ref, r_ref, *refs):
    raw_first, refs = Raw.take(plan, refs)
    raw_a, refs = Raw.take(plan, refs)
    raw_j, refs = Raw.take(plan, refs)
    a_ref, j_ref, f, ap, jq, x1, r, ah, u, w, jh, sems = refs
    place, copies = Place(plan), Copies(sems)
    raw_first, raw_a, raw_j = Raw(place, raw_first), Raw(place, raw_a), Raw(place, raw_j)
    usable = place.segment >= stride
    rows = ap.shape[0] // plan.panels
    load_ap = raw_a.start(copies, False, 1, ap)
    load_f = copies.start([(f_ref, f)])
    load_jq = copies.start([(jq_ref, jq)])
    load_x1 = copies.start([(x1_ref, x1)])
    load_r = copies.start([(r_ref, r)])
    load_jh = raw_j.start(copies, False, 2, jh, only_half=True)
    load_ah = raw_first.start(copies, True, 1, ah, 1, only_half=True)
    wait(load_ap + load_f + load_ah)
    pl.when(usable)(lambda: product(ah, f, ap))
    store_a = copies.start([(ah, a_ref)])
    wait(load_jq)
    pl.when(usable)(lambda: upper_rows(place, u, ap, jq))
    wait(load_x1)
    pl.when(usable)(lambda: product(w, u, x1))
    wait(load_r + load_jh)

    @pl.when(usable)
    def _():
        product(u, w, r)
        product(jh, u, ap, plus(jh))

    @pl.when(jnp.logical_not(usable))
    def _():
        for i, block in enumerate(place.part(True)):
            jh[i * rows : (i + 1) * rows, :] = jq[pl.ds(pl.multiple_of(block * rows, rows), rows), :]

    wait(copies.start([(jh, j_ref)]) + store_a)


def store_blocks(plan, copies, result, far, near):
    pairs = plan.half // 2
    rows = result.shape[0] // plan.half
    parts = len(far) // pairs
    stores = [
        (result.at[pl.ds((2 * (k % pairs) + 1) * rows + k // pairs * (rows // parts), rows // parts), :], piece)
        for k, piece in enumerate(far)
    ]
    stores += [(result.at[pl.ds(2 * i * rows, rows), :], piece) for i, piece in enumerate(near)]
    return copies.start(stores)


def front_kernel(plan, stride, c_mine, c_theirs, j_mine, j_theirs, a_mine, a_theirs, cq_mine, *refs):
    pairs = plan.half // 2
    far, near = refs[:pairs], refs[pairs : 2 * pairs]
    f_ref, x1_ref, r_ref, cp, jq, aq, ah, ch, x1, r, full, u, f, sems = refs[-14:]
    place, copies = Place(plan), Copies(sems)
    loads = [
        copies.start(full_pairs(place, c_mine, c_theirs, cp)),
        copies.start(full_pairs(place, j_mine, j_theirs, jq)),
        copies.start([(a_mine, ah)]),
        copies.start(full_pairs(place, a_mine, a_theirs, aq)),
        copies.start([(cq_mine, ch)]),
    ]
    stored = (x1_ref, r_ref, f_ref)
    stores = combine_front(place, copies, stride, loads, stored, cp, jq, aq, ah, ch, x1, r, full, u, f)
    wait(store_blocks(plan, copies, ch, far, near) + stores)


def trans_kernel(plan, stride, a_mine, a_theirs, f_ref, aq_mine, *refs):
    pairs = plan.half // 2
    c_near, far, near, refs = refs[:pairs], refs[pairs : 2 * pairs], refs[2 * pairs : 3 * pairs], refs[3 * pairs :]
    ap, f, ah, c, sems = refs
    place, copies = Place(plan), Copies(sems)
    rows = ah.shape[0] // plan.half
    usable = place.segment >= stride
    loads = copies.start([(f_ref, f), (aq_mine, ah)]) + copies.start(full_pairs(place, a_mine, a_theirs, ap))
    c_blocks = [c.at[pl.ds(i * rows, rows), :] for i in range(pairs)]
    load_c = copies.start(list(zip(c_near, c_blocks)))
    wait(loads)
    pl.when(usable)(lambda: product(ah, f, ap))
    stores = store_blocks(plan, copies, ah, far, [x.at[1] for x in near])
    wait(load_c)
    wait(copies.start([(block, x.at[0]) for block, x in zip(c_blocks, near)]) + stores)


def upper_kernel(plan, stride, a_mine, a_theirs, j_mine, j_theirs, x1_ref, r_ref, h_ref, ap, jq, x1, r, u, w, sems):
    place, copies = Place(plan), Copies(sems)

    @pl.when(place.segment >= stride)
    def _():
        load_ap = copies.start(full_pairs(place, a_mine, a_theirs, ap))
        load_jq = copies.start(full_pairs(place, j_mine, j_theirs, jq))
        load_x1 = copies.start([(x1_ref, x1)])
        load_r = copies.start([(r_ref, r)])
        wait(load_ap + load_jq)
        upper_rows(place, u, ap, jq)
        wait(load_x1)
        product(w, u, x1)
        wait(load_r)
        product(u, w, r)
        wait(copies.start([(u, h_ref)]))


def info_kernel(plan, stride, h_ref, a_mine, a_theirs, jp_mine, jq_mine, *refs):
    pairs = plan.half // 2
    far, near = refs[:pairs], refs[pairs : 2 * pairs]
    h, ap, jh, sems = refs[-4:]
    place, copies = Place(plan), Copies(sems)
    usable = place.segment >= stride
    load_jh = copies.start_either(usable, [(jp_mine, jh)], [(jq_mine, jh)])
    wait(load_jh + copies.start([(h_ref, h)]) + copies.start(full_pairs(place, a_mine, a_theirs, ap)))
    pl.when(usable)(lambda: product(jh, h, ap, plus(jh)))
    wait(store_blocks(plan, copies, jh, far, near))


def home_blocks(plan, rows):
    half, pairs = plan.half, plan.half // 2
    t, z = lax.axis_index("tm"), lax.axis_index("panel")
    tests = []
    for segment, panel in ((t, z), (plan.groups - 1 - t, plan.panels - 1 - z)):
        distance = lax.rem(panel + half - lax.rem(segment, 2), half)
        which = jnp.where(panel >= half, lax.rem(panel, pairs), pairs + lax.rem(distance, pairs))
        tests.append(which)
    return tests


def home_kernel(plan, *refs):
    half, pairs = plan.half, plan.half // 2
    c_far, a_far, ca_near = [refs[i * pairs : (i + 1) * pairs] for i in range(3)]
    outs, (held, sems) = refs[3 * pairs : 3 * pairs + 2], refs[3 * pairs + 2 :]
    rows = held.shape[2]
    waits = []
    for k, which in enumerate(home_blocks(plan, rows)):
        c, a = held.at[k, 0], held.at[k, 1]
        for i in range(pairs):
            far = [(c_far[i], c, 0), (a_far[i], a, 1)]
            near = [(ca_near[i].at[0], c, 0), (ca_near[i].at[1], a, 1)]
            for owner, moves in ((i, far), (pairs + i, near)):
                for source, target, matrix in moves:
                    pl.when(which == owner)(pltpu.make_async_copy(source, target, sems.at[2 * k + matrix]).start)
        for matrix in range(2):
            waits.append(pltpu.make_async_copy(a_far[0], held.at[k, matrix], sems.at[2 * k + matrix]))
    wait(waits)
    run = [pltpu.make_async_copy(held.at[k], outs[k].at[pl.ds(0, 2)], sems.at[k]) for k in range(2)]
    for copy in run:
        copy.start()
    wait(run)


def home_info_kernel(plan, f_in, b_in, *refs):
    pairs = plan.half // 2
    j_far, j_near, outs, (held, sems) = refs[:pairs], refs[pairs : 2 * pairs], refs[2 * pairs : 2 * pairs + 2], refs[-2:]
    waits, run = [], []
    for k, which in enumerate(home_blocks(plan, held.shape[1])):
        for owner, source in enumerate([*j_far, *j_near]):
            pl.when(which == owner)(pltpu.make_async_copy(source, held.at[k], sems.at[k]).start)
        waits.append(pltpu.make_async_copy(j_far[0], held.at[k], sems.at[k]))
        run.append(pltpu.make_async_copy(held.at[k], outs[k].at[2], sems.at[2 + k]))
    for copy, store in zip(waits, run):
        copy.wait()
        store.start()
    wait(run)


def after(x, *others):
    return lax.optimization_barrier((x, *others))[0]


def shards(plan, forward_element, backward_element):
    forward, backward = forward_element[:, 0], backward_element[:, 0]
    rows, n = forward.shape[1:]
    half = plan.half
    full, part, block = bf16(n, n), bf16(n // 2, n), bf16(rows, n)
    square, slab = pltpu.VMEM((n, n), jnp.bfloat16), pltpu.VMEM((n // 2, n), jnp.bfloat16)
    sems = pltpu.SemaphoreType.DMA((12 * half,))

    def send(x, routes):
        return lax.ppermute(x, AXES, routes)

    def swap(x):
        return send(x, plan.core)

    def kernel(body, outs, operands, scratch, **options):
        return call(functools.partial(body, plan, *options.pop("static", ())), outs, operands, [*scratch, sems], **options)

    t, z = lax.axis_index("tm"), lax.axis_index("panel")
    layer = jnp.where(z < half, z, plan.panels - 1 - z)
    core = jnp.where(z < half, t, plan.groups - 1 - t) % 2
    is_q, special = (core + layer) % 2 == 0, (core == 1) & (layer == 0)
    other_c = jnp.where(z < half, backward[0], forward[0])
    other_ja = jnp.stack([jnp.where(z < half, backward[i], forward[i]) for i in (2, 1)])
    own = jnp.where(z < half, forward, backward)

    far_c = [send(other_c, route) for route in plan.cross]
    far_ja = [send(other_ja, route) for route in plan.cross]
    local = [send(own, plan.gather[d]) for d in range(1, half)]
    onward_local = send(after(own, *far_c), plan.onward)
    far_c_of_p = [send(x, plan.forward) for x in far_c]
    far_first = [jnp.where(is_q, q, p[None]) for q, p in zip(far_ja, far_c_of_p)]
    first_swap = [swap(x) for x in far_first]
    near = [jnp.where(special, onward_local, own), *local]
    near_swap = [swap(x) for x in near]
    nears = [*near, *near_swap]
    raw_first = [*nears, *far_first, *first_swap]
    kept_c = [swap(x) for x in far_c[: half // 2]]

    rest = [send(x, plan.forward) for x in far_ja]

    c_new, jq, x1, r, f = kernel(
        first_kernel,
        [part, full, full, full, part],
        [*raw_first, *kept_c, *far_c[half // 2 :]],
        [square] * 3 + [slab] * 2 + [square] * 3 + [slab] * 2,
        static=(1,),
    )
    rest = [after(x, c_new) for x in rest]
    j_rest, a_rest = [x[0] for x in rest], [x[1] for x in rest]
    raw_rest = [*nears, *a_rest, *[swap(x) for x in a_rest], *nears, *j_rest, *[swap(x) for x in j_rest]]
    a_new, j_new = kernel(
        trans_info_kernel,
        [part] * 2,
        [after(f, c_new), jq, x1, r, *raw_first, *raw_rest],
        [slab] + [square] * 4 + [slab] * 4,
        static=(1,),
    )
    j_swap, a_swap = swap(j_new), swap(a_new)
    c_next = send(c_new, plan.next)
    c_next, a_new = lax.optimization_barrier((c_next, a_new))
    c_next_swap = swap(c_next)
    a_next = send(a_new, plan.next)

    pairs = range(half // 2)
    blocks = [block for _ in pairs]
    far, near = [plan.home[True, i] for i in pairs], [plan.home[False, i] for i in pairs]

    def send_home(pieces, routes):
        return [send(x, route) for x, route in zip(pieces, routes)]

    *c_pieces, f, x1, r = kernel(
        front_kernel,
        [*blocks, *blocks, part, full, full],
        [c_next, c_next_swap, j_new, j_swap, a_new, a_swap, c_new],
        [square] * 3 + [slab] * 2 + [square] * 3 + [slab] * 2,
        static=(2,),
    )
    c_far, c_near = send_home(c_pieces[: half // 2], far), c_pieces[half // 2 :]
    j_next = send(after(j_new, a_next), plan.next)
    a_next = after(a_next, f, *c_far)
    a_next_swap = swap(a_next)
    a_pieces = kernel(
        trans_kernel,
        [*blocks, *[bf16(2, rows, n) for _ in pairs]],
        [a_next, a_next_swap, f, a_new, *c_near],
        [square] + [slab] * 3,
        static=(2,),
    )
    a_far = send_home(a_pieces[: half // 2], far)
    ca_near = send_home(a_pieces[half // 2 :], near)
    (h,) = kernel(
        upper_kernel,
        [part],
        [a_next, a_next_swap, j_new, j_swap, after(x1, *a_pieces), r],
        [square] * 4 + [slab] * 2,
        static=(2,),
    )
    j_pieces = kernel(
        info_kernel,
        [*blocks, *blocks],
        [h, a_next, a_next_swap, after(j_next, h), j_new],
        [slab, square, slab],
        static=(2,),
    )
    j_home = send_home([after(x, *a_far, *ca_near) for x in j_pieces], [*far, *near])

    outs = [bf16(3, rows, n)] * 2
    f_out, b_out = kernel(
        home_kernel,
        outs,
        [*c_far, *a_far, *ca_near],
        [pltpu.VMEM((2, 2, rows, n), jnp.bfloat16)],
        flops=n**3,
    )
    f_out, b_out = kernel(
        home_info_kernel,
        outs,
        [f_out, b_out, *j_home],
        [pltpu.VMEM((2, rows, n), jnp.bfloat16)],
        aliases={0: 0, 1: 1},
    )
    return f_out[:, None], b_out[:, None]


def solution(mesh):
    plan = Plan(mesh.shape["tm"], mesh.shape["panel"])
    spec = P(None, "tm", "panel", None)
    return jax.shard_map(
        functools.partial(shards, plan),
        mesh=mesh,
        in_specs=(spec, spec),
        out_specs=(spec, spec),
        check_vma=False,
    )
```

```python
import functools

import jax
import jax.numpy as jnp
from jax import lax
from jax.experimental import pallas as pl
from jax.experimental.pallas import tpu as pltpu
from jax.sharding import PartitionSpec as P

AXES = ("tm", "panel")
VMEM_BYTES = 32 * 2**20
TILE = 512
HBM = pl.BlockSpec(memory_space=pltpu.HBM)


class Plan:
    def __init__(self, groups, panels):
        self.groups, self.panels, self.half = groups, panels, panels // 2
        assert groups % 2 == 0 and panels % 4 == 0
        columns = range(groups // 2)
        half = self.half

        def table(forward_routes):
            last = groups * panels - 1
            routes = [(a * panels + b, c * panels + d) for (a, b), (c, d) in forward_routes]
            return routes + [(last - source, last - target) for source, target in routes]

        def in_range(routes):
            return [route for route in routes if route[1][0] < groups]

        everyone = [(t, z) for t in range(groups) for z in range(panels)]
        self.core = [(t * panels + z, (t ^ 1) * panels + z) for t, z in everyone]
        q_of = {t: (t, t % 2) for t in range(groups)}
        p_of = {t: (t, 1) if t % 2 == 0 else (t + 2, 0) for t in range(groups)}
        self.cross = [table([((t, half + q), q_of[t]) for t in range(groups)]) for q in range(half)]
        self.forward = table(in_range([(q_of[t], p_of[t]) for t in range(groups)]))
        self.gather = {}
        for d in range(1, half):
            routes = [((t, (q_of[t][1] + d) % half), q_of[t]) for t in range(groups)]
            routes += [((t, (p_of[t][1] + d) % half), p_of[t]) for t in range(groups)]
            self.gather[d] = table(in_range(routes))
        self.onward = table(in_range([((t, 0), p_of[t]) for t in range(1, groups, 2)]))
        active = [(2 * c + core, layer) for c in columns for core in (0, 1) for layer in (0, 1)]
        self.next = table(in_range([((t, z), (t + 2, z)) for t, z in active]))
        self.home = {}
        for far in (True, False):
            for i in range(half // 2):
                routes = []
                for t, z in active:
                    d = i + (half // 2 if (t + z) % 2 == 0 else 0)
                    routes.append(((t, z), (t - t % 2 + z, half + d if far else (z + d) % half)))
                self.home[far, i] = table(routes)


class Place:
    def __init__(self, plan):
        t, z = lax.axis_index("tm"), lax.axis_index("panel")
        self.plan = plan
        self.forward = z < plan.half
        self.layer = jnp.where(self.forward, z, plan.panels - 1 - z)
        self.t = jnp.where(self.forward, t, plan.groups - 1 - t)
        core = lax.rem(self.t, 2)
        self.is_q = lax.rem(core + self.layer, 2) == 0
        self.is_p = jnp.logical_not(self.is_q)
        self.segment = self.t - core + self.layer

    def near(self, d):
        layer = lax.rem(self.layer + d, self.plan.half)
        return jnp.where(self.forward, layer, self.plan.panels - 1 - layer)

    def far(self, q):
        half = self.plan.half
        return jnp.where(self.forward, half + q, half - 1 - q)

    def part(self, mine):
        pairs = self.plan.half // 2
        first = jnp.where(self.is_q == mine, pairs, 0)
        return [block for i in range(pairs) for block in (self.near(first + i), self.far(first + i))]


def call(kernel, out_shapes, operands, scratch=(), flops=1, aliases=None):
    return pl.pallas_call(
        kernel,
        out_shape=list(out_shapes),
        in_specs=[HBM] * len(operands),
        out_specs=[HBM] * len(out_shapes),
        input_output_aliases=aliases or {},
        scratch_shapes=list(scratch),
        compiler_params=pltpu.CompilerParams(vmem_limit_bytes=VMEM_BYTES),
        cost_estimate=pl.CostEstimate(flops=flops, bytes_accessed=1, transcendentals=0),
    )(*operands)


def bf16(*shape):
    return jax.ShapeDtypeStruct(shape, jnp.bfloat16)


def band(ref, block, rows):
    start = block * rows
    return ref.at[pl.ds(start if isinstance(block, int) else pl.multiple_of(start, rows), rows), :]


class Copies:
    def __init__(self, sems):
        self.sems, self.count = sems, 0

    def start(self, pairs, condition=None):
        copies = [pltpu.make_async_copy(a, b, self.sems.at[self.count + i]) for i, (a, b) in enumerate(pairs)]
        self.count += len(copies)
        self._start(copies, condition)
        return copies

    def start_either(self, condition, pairs, other_pairs):
        first = self.count
        copies = self.start(pairs, condition)
        self.count = first
        self.start(other_pairs, jnp.logical_not(condition))
        return copies

    @staticmethod
    def _start(copies, condition):
        def run():
            for copy in copies:
                copy.start()

        run() if condition is None else pl.when(condition)(run)


def wait(copies):
    for copy in copies:
        copy.wait()


def full_pairs(place, mine, theirs, target):
    rows = target.shape[0] // place.plan.panels
    return [
        (band(half, i, rows), band(target, block, rows))
        for half, is_mine in ((mine, True), (theirs, False))
        for i, block in enumerate(place.part(is_mine))
    ]


class Raw:
    def __init__(self, place, refs):
        half = place.plan.half
        self.place = place
        self.near = {True: refs[:half], False: refs[half : 2 * half]}
        self.far = {True: refs[2 * half : 3 * half], False: refs[3 * half : 4 * half]}

    @staticmethod
    def take(plan, refs):
        return refs[: 4 * plan.half], refs[4 * plan.half :]

    def start(self, copies, of_q, index, target, far_index=None, only_half=False):
        place, half = self.place, self.place.plan.half
        rows = self.near[True][0].shape[1]

        def pairs(mine):
            on_q = of_q == mine
            result = []
            ds = range(half // 2 if on_q else 0, half if on_q else half // 2) if only_half else range(half)
            for i, d in enumerate(ds):
                near, far = (2 * i, 2 * i + 1) if only_half else (place.near(d), place.far(d))
                result.append((self.near[mine][d].at[index], band(target, near, rows)))
                far_ref = self.far[mine][d] if far_index is None else self.far[mine][d].at[far_index]
                result.append((far_ref, band(target, far, rows)))
            return result

        return copies.start_either(place.is_q if of_q else place.is_p, pairs(True), pairs(False))


def product(out, a, b, finish=lambda acc, rows: acc, b_transposed=False, tile=TILE):
    n = out.shape[0]
    tile = min(tile, n)
    dims = (((1,), (1 if b_transposed else 0,)), ((), ()))

    @pl.loop(0, n // tile)
    def _(i):
        rows = pl.ds(pl.multiple_of(i * tile, tile), tile)
        acc = lax.dot_general(a[rows, :], b[...], dims, preferred_element_type=jnp.float32)
        out[rows, :] = finish(acc, rows).astype(jnp.bfloat16)


def upper_rows(place, out, a, b):
    rows = a.shape[0] // place.plan.panels
    for i, block in enumerate(place.part(True)):
        columns = pl.ds(pl.multiple_of(block * rows, rows), rows)
        acc = lax.dot_general(a[:, columns], b[...], (((0,), (0,)), ((), ())), preferred_element_type=jnp.float32)
        out[i * rows : (i + 1) * rows, :] = acc.astype(jnp.bfloat16)


def identity(rows, n):
    shape = (rows.size, n)
    row = lax.broadcasted_iota(jnp.int32, shape, 0) + rows.start
    return (row == lax.broadcasted_iota(jnp.int32, shape, 1)).astype(jnp.float32)


def iterates(n, cp, jq, u, x1, r):
    def first_iterate(acc, rows):
        x1[rows, :] = (identity(rows, n) - acc.astype(jnp.bfloat16)).astype(jnp.bfloat16)
        return acc

    product(u, cp, jq, first_iterate, tile=n)
    product(r, u, x1, lambda acc, rows: identity(rows, n) + u[rows, :] - acc, tile=n)


def plus(ref):
    return lambda acc, rows: acc + ref[rows, :]


def combine_front(place, copies, stride, loads, stored, cp, jq, aq, ah, ch, x1, r, full, u, f):
    load_cp, load_jq, load_ah, load_aq, load_ch = loads
    usable = place.segment >= stride
    wait(load_cp + load_jq)
    pl.when(usable)(lambda: iterates(cp.shape[0], cp, jq, full, x1, r))
    stores = copies.start(list(zip((x1, r), stored)))
    wait(load_ah)

    @pl.when(usable)
    def _():
        product(u, ah, x1)
        product(f, u, r)

    stores += copies.start([(f, stored[2])])
    pl.when(usable)(lambda: product(u, f, cp))
    wait(load_aq + load_ch)
    pl.when(usable)(lambda: product(ch, u, aq, plus(ch), b_transposed=True))
    return stores


def first_kernel(plan, stride, *refs):
    pairs = plan.half // 2
    raw, refs = Raw.take(plan, refs)
    kept, late, refs = refs[:pairs], refs[pairs : 2 * pairs], refs[2 * pairs :]
    c_ref, jq_ref, x1_ref, r_ref, f_ref, cp, jq, aq, ah, ch, x1, r, full, u, f, sems = refs
    place, copies = Place(plan), Copies(sems)
    raw_c = Raw(place, [*raw[: 2 * plan.half], *late, *late, *kept, *late])
    raw = Raw(place, raw)
    loads = [
        raw.start(copies, False, 0, cp, 0),
        raw.start(copies, True, 2, jq, 0),
        raw.start(copies, True, 1, ah, 1, only_half=True),
        raw.start(copies, True, 1, aq, 1),
        raw_c.start(copies, True, 0, ch, only_half=True),
    ]
    stored = (x1_ref, r_ref, f_ref)
    stores = combine_front(place, copies, stride, loads, stored, cp, jq, aq, ah, ch, x1, r, full, u, f)
    wait(stores + copies.start([(ch, c_ref), (jq, jq_ref)]))


def trans_info_kernel(plan, stride, f_ref, jq_ref, x1_ref, r_ref, *refs):
    raw_first, refs = Raw.take(plan, refs)
    raw_a, refs = Raw.take(plan, refs)
    raw_j, refs = Raw.take(plan, refs)
    a_ref, j_ref, f, ap, jq, x1, r, ah, u, w, jh, sems = refs
    place, copies = Place(plan), Copies(sems)
    raw_first, raw_a, raw_j = Raw(place, raw_first), Raw(place, raw_a), Raw(place, raw_j)
    usable = place.segment >= stride
    rows = ap.shape[0] // plan.panels
    load_ap = raw_a.start(copies, False, 1, ap)
    load_f = copies.start([(f_ref, f)])
    load_jq = copies.start([(jq_ref, jq)])
    load_x1 = copies.start([(x1_ref, x1)])
    load_r = copies.start([(r_ref, r)])
    load_jh = raw_j.start(copies, False, 2, jh, only_half=True)
    load_ah = raw_first.start(copies, True, 1, ah, 1, only_half=True)
    wait(load_ap + load_f + load_ah)
    pl.when(usable)(lambda: product(ah, f, ap))
    store_a = copies.start([(ah, a_ref)])
    wait(load_jq)
    pl.when(usable)(lambda: upper_rows(place, u, ap, jq))
    wait(load_x1)
    pl.when(usable)(lambda: product(w, u, x1))
    wait(load_r + load_jh)

    @pl.when(usable)
    def _():
        product(u, w, r)
        product(jh, u, ap, plus(jh))

    @pl.when(jnp.logical_not(usable))
    def _():
        for i, block in enumerate(place.part(True)):
            jh[i * rows : (i + 1) * rows, :] = jq[pl.ds(pl.multiple_of(block * rows, rows), rows), :]

    wait(copies.start([(jh, j_ref)]) + store_a)


def store_blocks(plan, copies, result, far, near):
    pairs = plan.half // 2
    rows = result.shape[0] // plan.half
    parts = len(far) // pairs
    stores = [
        (result.at[pl.ds((2 * (k % pairs) + 1) * rows + k // pairs * (rows // parts), rows // parts), :], piece)
        for k, piece in enumerate(far)
    ]
    stores += [(result.at[pl.ds(2 * i * rows, rows), :], piece) for i, piece in enumerate(near)]
    return copies.start(stores)


def front_kernel(plan, stride, c_mine, c_theirs, j_mine, j_theirs, a_mine, a_theirs, cq_mine, *refs):
    pairs = plan.half // 2
    far, near = refs[:pairs], refs[pairs : 2 * pairs]
    f_ref, x1_ref, r_ref, cp, jq, aq, ah, ch, x1, r, full, u, f, sems = refs[-14:]
    place, copies = Place(plan), Copies(sems)
    loads = [
        copies.start(full_pairs(place, c_mine, c_theirs, cp)),
        copies.start(full_pairs(place, j_mine, j_theirs, jq)),
        copies.start([(a_mine, ah)]),
        copies.start(full_pairs(place, a_mine, a_theirs, aq)),
        copies.start([(cq_mine, ch)]),
    ]
    stored = (x1_ref, r_ref, f_ref)
    stores = combine_front(place, copies, stride, loads, stored, cp, jq, aq, ah, ch, x1, r, full, u, f)
    wait(store_blocks(plan, copies, ch, far, near) + stores)


def trans_kernel(plan, stride, a_mine, a_theirs, f_ref, aq_mine, *refs):
    pairs = plan.half // 2
    c_near, far, near, refs = refs[:pairs], refs[pairs : 2 * pairs], refs[2 * pairs : 3 * pairs], refs[3 * pairs :]
    ap, f, ah, c, sems = refs
    place, copies = Place(plan), Copies(sems)
    rows = ah.shape[0] // plan.half
    usable = place.segment >= stride
    loads = copies.start([(f_ref, f), (aq_mine, ah)]) + copies.start(full_pairs(place, a_mine, a_theirs, ap))
    c_blocks = [c.at[pl.ds(i * rows, rows), :] for i in range(pairs)]
    load_c = copies.start(list(zip(c_near, c_blocks)))
    wait(loads)
    pl.when(usable)(lambda: product(ah, f, ap))
    stores = store_blocks(plan, copies, ah, far, [x.at[1] for x in near])
    wait(load_c)
    wait(copies.start([(block, x.at[0]) for block, x in zip(c_blocks, near)]) + stores)


def upper_kernel(plan, stride, a_mine, a_theirs, j_mine, j_theirs, x1_ref, r_ref, h_ref, ap, jq, x1, r, u, w, sems):
    place, copies = Place(plan), Copies(sems)

    @pl.when(place.segment >= stride)
    def _():
        load_ap = copies.start(full_pairs(place, a_mine, a_theirs, ap))
        load_jq = copies.start(full_pairs(place, j_mine, j_theirs, jq))
        load_x1 = copies.start([(x1_ref, x1)])
        load_r = copies.start([(r_ref, r)])
        wait(load_ap + load_jq)
        upper_rows(place, u, ap, jq)
        wait(load_x1)
        product(w, u, x1)
        wait(load_r)
        product(u, w, r)
        wait(copies.start([(u, h_ref)]))


def info_kernel(plan, stride, h_ref, a_mine, a_theirs, jp_mine, jq_mine, *refs):
    pairs = plan.half // 2
    far, near = refs[:pairs], refs[pairs : 2 * pairs]
    h, ap, jh, sems = refs[-4:]
    place, copies = Place(plan), Copies(sems)
    usable = place.segment >= stride
    load_jh = copies.start_either(usable, [(jp_mine, jh)], [(jq_mine, jh)])
    wait(load_jh + copies.start([(h_ref, h)]) + copies.start(full_pairs(place, a_mine, a_theirs, ap)))
    pl.when(usable)(lambda: product(jh, h, ap, plus(jh)))
    wait(store_blocks(plan, copies, jh, far, near))


def home_blocks(plan, rows):
    half, pairs = plan.half, plan.half // 2
    t, z = lax.axis_index("tm"), lax.axis_index("panel")
    tests = []
    for segment, panel in ((t, z), (plan.groups - 1 - t, plan.panels - 1 - z)):
        distance = lax.rem(panel + half - lax.rem(segment, 2), half)
        which = jnp.where(panel >= half, lax.rem(panel, pairs), pairs + lax.rem(distance, pairs))
        tests.append(which)
    return tests


def home_kernel(plan, *refs):
    half, pairs = plan.half, plan.half // 2
    c_far, a_far, ca_near = [refs[i * pairs : (i + 1) * pairs] for i in range(3)]
    outs, (held, sems) = refs[3 * pairs : 3 * pairs + 2], refs[3 * pairs + 2 :]
    rows = held.shape[2]
    waits = []
    for k, which in enumerate(home_blocks(plan, rows)):
        c, a = held.at[k, 0], held.at[k, 1]
        for i in range(pairs):
            far = [(c_far[i], c, 0), (a_far[i], a, 1)]
            near = [(ca_near[i].at[0], c, 0), (ca_near[i].at[1], a, 1)]
            for owner, moves in ((i, far), (pairs + i, near)):
                for source, target, matrix in moves:
                    pl.when(which == owner)(pltpu.make_async_copy(source, target, sems.at[2 * k + matrix]).start)
        for matrix in range(2):
            waits.append(pltpu.make_async_copy(a_far[0], held.at[k, matrix], sems.at[2 * k + matrix]))
    wait(waits)
    run = [pltpu.make_async_copy(held.at[k], outs[k].at[pl.ds(0, 2)], sems.at[k]) for k in range(2)]
    for copy in run:
        copy.start()
    wait(run)


def home_info_kernel(plan, f_in, b_in, *refs):
    pairs = plan.half // 2
    j_far, j_near, outs, (held, sems) = refs[:pairs], refs[pairs : 2 * pairs], refs[2 * pairs : 2 * pairs + 2], refs[-2:]
    waits, run = [], []
    for k, which in enumerate(home_blocks(plan, held.shape[1])):
        for owner, source in enumerate([*j_far, *j_near]):
            pl.when(which == owner)(pltpu.make_async_copy(source, held.at[k], sems.at[k]).start)
        waits.append(pltpu.make_async_copy(j_far[0], held.at[k], sems.at[k]))
        run.append(pltpu.make_async_copy(held.at[k], outs[k].at[2], sems.at[2 + k]))
    for copy, store in zip(waits, run):
        copy.wait()
        store.start()
    wait(run)


def after(x, *others):
    return lax.optimization_barrier((x, *others))[0]


def shards(plan, forward_element, backward_element):
    forward, backward = forward_element[:, 0], backward_element[:, 0]
    rows, n = forward.shape[1:]
    half = plan.half
    full, part, block = bf16(n, n), bf16(n // 2, n), bf16(rows, n)
    square, slab = pltpu.VMEM((n, n), jnp.bfloat16), pltpu.VMEM((n // 2, n), jnp.bfloat16)
    sems = pltpu.SemaphoreType.DMA((12 * half,))

    def send(x, routes):
        return lax.ppermute(x, AXES, routes)

    def swap(x):
        return send(x, plan.core)

    def kernel(body, outs, operands, scratch, **options):
        return call(functools.partial(body, plan, *options.pop("static", ())), outs, operands, [*scratch, sems], **options)

    t, z = lax.axis_index("tm"), lax.axis_index("panel")
    layer = jnp.where(z < half, z, plan.panels - 1 - z)
    core = jnp.where(z < half, t, plan.groups - 1 - t) % 2
    is_q, special = (core + layer) % 2 == 0, (core == 1) & (layer == 0)
    other_c = jnp.where(z < half, backward[0], forward[0])
    other_ja = jnp.stack([jnp.where(z < half, backward[i], forward[i]) for i in (2, 1)])
    own = jnp.where(z < half, forward, backward)

    far_c = [send(other_c, route) for route in plan.cross]
    far_ja = [send(other_ja, route) for route in plan.cross]
    local = [send(own, plan.gather[d]) for d in range(1, half)]
    onward_local = send(after(own, *far_c), plan.onward)
    far_c_of_p = [send(x, plan.forward) for x in far_c]
    far_first = [jnp.where(is_q, q, p[None]) for q, p in zip(far_ja, far_c_of_p)]
    first_swap = [swap(x) for x in far_first]
    near = [jnp.where(special, onward_local, own), *local]
    near_swap = [swap(x) for x in near]
    nears = [*near, *near_swap]
    raw_first = [*nears, *far_first, *first_swap]
    kept_c = [swap(x) for x in far_c[: half // 2]]

    rest = [send(x, plan.forward) for x in far_ja]

    c_new, jq, x1, r, f = kernel(
        first_kernel,
        [part, full, full, full, part],
        [*raw_first, *kept_c, *far_c[half // 2 :]],
        [square] * 3 + [slab] * 2 + [square] * 3 + [slab] * 2,
        static=(1,),
    )
    rest = [after(x, c_new) for x in rest]
    j_rest, a_rest = [x[0] for x in rest], [x[1] for x in rest]
    raw_rest = [*nears, *a_rest, *[swap(x) for x in a_rest], *nears, *j_rest, *[swap(x) for x in j_rest]]
    a_new, j_new = kernel(
        trans_info_kernel,
        [part] * 2,
        [after(f, c_new), jq, x1, r, *raw_first, *raw_rest],
        [slab] + [square] * 4 + [slab] * 4,
        static=(1,),
    )
    j_swap, a_swap = swap(j_new), swap(a_new)
    c_next = send(c_new, plan.next)
    c_next, a_new = lax.optimization_barrier((c_next, a_new))
    c_next_swap = swap(c_next)
    a_next = send(a_new, plan.next)

    pairs = range(half // 2)
    blocks = [block for _ in pairs]
    far, near = [plan.home[True, i] for i in pairs], [plan.home[False, i] for i in pairs]

    def send_home(pieces, routes):
        return [send(x, route) for x, route in zip(pieces, routes)]

    *c_pieces, f, x1, r = kernel(
        front_kernel,
        [*blocks, *blocks, part, full, full],
        [c_next, c_next_swap, j_new, j_swap, a_new, a_swap, c_new],
        [square] * 3 + [slab] * 2 + [square] * 3 + [slab] * 2,
        static=(2,),
    )
    c_far, c_near = send_home(c_pieces[: half // 2], far), c_pieces[half // 2 :]
    j_next = send(after(j_new, f), plan.next)
    a_next = after(a_next, f, *c_far)
    a_next_swap = swap(a_next)
    a_pieces = kernel(
        trans_kernel,
        [*blocks, *[bf16(2, rows, n) for _ in pairs]],
        [a_next, a_next_swap, f, a_new, *c_near],
        [square] + [slab] * 3,
        static=(2,),
    )
    a_far = send_home(a_pieces[: half // 2], far)
    ca_near = send_home(a_pieces[half // 2 :], near)
    (h,) = kernel(
        upper_kernel,
        [part],
        [a_next, a_next_swap, j_new, j_swap, after(x1, *a_pieces), r],
        [square] * 4 + [slab] * 2,
        static=(2,),
    )
    j_pieces = kernel(
        info_kernel,
        [*blocks, *blocks],
        [h, a_next, a_next_swap, after(j_next, h), j_new],
        [slab, square, slab],
        static=(2,),
    )
    j_home = send_home([after(x, *a_far, *ca_near) for x in j_pieces], [*far, *near])

    outs = [bf16(3, rows, n)] * 2
    f_out, b_out = kernel(
        home_kernel,
        outs,
        [*c_far, *a_far, *ca_near],
        [pltpu.VMEM((2, 2, rows, n), jnp.bfloat16)],
        flops=n**3,
    )
    f_out, b_out = kernel(
        home_info_kernel,
        outs,
        [f_out, b_out, *j_home],
        [pltpu.VMEM((2, rows, n), jnp.bfloat16)],
        aliases={0: 0, 1: 1},
    )
    return f_out[:, None], b_out[:, None]


def solution(mesh):
    plan = Plan(mesh.shape["tm"], mesh.shape["panel"])
    spec = P(None, "tm", "panel", None)
    return jax.shard_map(
        functools.partial(shards, plan),
        mesh=mesh,
        in_specs=(spec, spec),
        out_specs=(spec, spec),
        check_vma=False,
    )
```
